32 devices in a mesh: section: 8 (over y, x, core), peer: 4 (over z).
Axes of the slice: x: 2, y: 2, z: 4, core: 2. Of those that a mesh axis runs over, the one named last changes fastest.
Arguments:
- inputs: bfloat16 [8, 4, 128, 5120], P('section', 'peer'), may hold values from -6 to 6
- out_grad: bfloat16 [8, 4, 128, 5120], P('section', 'peer'), may hold values from -6 to 6
- gains: float32 [8, 5120], P('section'), may hold values from 0.1 to 1.9
- down_proj: bfloat16 [8, 5120, 128], P('section'), may hold values from -0.078125 to 0.078125
- up_proj: bfloat16 [8, 128, 5120], P('section'), may hold values from -0.5 to 0.5
- wiring: int32 [8, 4, 4], replicated, may hold values from 0 to 2, as said below
- pair_mask: int32 [8], replicated, may hold values from 1 to 3
Outputs:
- next_inputs: bfloat16 [8, 4, 128, 5120], P('section', 'peer')
- returned_grad: bfloat16 [8, 4, 128, 5120], P('section', 'peer')
- grad_down: float32 [8, 4, 5120, 128], P('section', 'peer')
- grad_up: float32 [8, 4, 128, 5120], P('section', 'peer')
The draws below stay inside these ranges and needn't reach their ends.
Inputs may be any that keep to these rules, and one draw needn't show every extreme that they name: For each section, every row and every column of wiring sums to 4; entries are 0, 1 or 2, and 2 occurs in every row and every column. `pair_mask`: 4 is a power of two; each section's mask is nonzero.
All inputs are finite; a program needn't handle non-finite values.
Results may differ from the reference program's by a relative error of at most 0.006.
Values may be sent and summed in bfloat16 or wider, within the bound.
No kernel may reach another device: no remote copies, remote signals or barrier semaphores. Data moves between devices by JAX's collectives and lax.ppermute only.
A program may use at most 128 MiB of HBM per device.

```python
import jax
import jax.numpy as jnp
from jax import lax

D = 5120
R = 128
TOK = 128
NB = 4
BLK = 32
SECTIONS = 8
PEERS = 4


def draw_wiring(key, part):
    keys = jax.random.split(jax.random.fold_in(key, 17), SECTIONS)

    def one_section(section_key):
        key_a, key_b = jax.random.split(section_key)
        order = jax.random.permutation(key_a, PEERS)
        shifts = jax.random.permutation(key_b, PEERS)
        rows = jnp.arange(PEERS, dtype=jnp.int32)
        cols = jnp.arange(PEERS, dtype=jnp.int32)
        total = jnp.zeros((PEERS, PEERS), jnp.int32)
        heavy = PEERS // 4
        light = PEERS // 2
        for index in range(heavy + light):
            weight = 2 if index < heavy else 1
            target = order[(rows + shifts[index]) % PEERS]
            total = total + weight * (target[:, None] == cols[None, :]).astype(jnp.int32)
        return total
    return jax.vmap(one_section)(keys).astype(jnp.int32)


def place_ends(drawn, stream_key, smallest, top_value):
    extent = drawn.shape
    spot = [jax.random.randint(jax.random.fold_in(stream_key, axis), (), 0, extent[axis]) for axis in range(len(extent))]
    drawn = drawn.at[tuple(spot)].set(smallest)
    longest = extent.index(max(extent))
    spot[longest] = (spot[longest] + 1) % extent[longest]
    return drawn.at[tuple(spot)].set(top_value)


def levels(rng, shape, cuts, least, high):
    level, own = 1.0, jax.random.fold_in(rng, 6)
    for dim, blocks in cuts:
        heights = jnp.exp(jax.random.uniform(jax.random.fold_in(own, dim), (blocks,), jnp.float32, least / len(cuts), high / len(cuts)))
        level = level * jnp.repeat(heights, shape[dim] // blocks).reshape([-1 if axis == dim else 1 for axis in range(len(shape))])
    return level


def noise(rng, dims, deviation, most, cuts=(), kind=jnp.bfloat16):
    loudness = levels(rng, dims, cuts, -0.22, 0.18) if cuts else 1.0
    values = jax.random.normal(rng, dims, jnp.float32) * deviation * loudness
    return jnp.minimum(jnp.maximum(values, -most), most).astype(kind)


def setup_inputs(seed: int = 0) -> dict:
    key_of = jax.random.split(jax.random.key(seed), 8)
    return {
        "inputs": noise(key_of[0], (SECTIONS, PEERS, TOK, D), 1.0, 6.0, ((0, 8), (1, 4))),
        "out_grad": noise(key_of[1], (SECTIONS, PEERS, TOK, D), 1.0, 6.0, ((0, 8), (1, 4))),
        "gains": jnp.clip(1.0 + 0.18 * jax.random.normal(key_of[2], (SECTIONS, D), jnp.float32), 0.1, 1.9),
        "down_proj": noise(key_of[3], (SECTIONS, D, R), D ** -0.5, 0.078125, ((0, 8),)),
        "up_proj": noise(key_of[4], (SECTIONS, R, D), R ** -0.5, 0.5, ((0, 8),)),
        "wiring": draw_wiring(jax.random.fold_in(key_of[7], 71), 0),
        "pair_mask": place_ends(jax.random.randint(key_of[6], (SECTIONS,), 1, PEERS), jax.random.fold_in(key_of[6], 1), 1, PEERS - 1).astype(jnp.int32),
    }


def layer(x, dy, g, down, up):
    xf = x.astype(jnp.float32)
    ms = lax.optimization_barrier(jnp.mean(xf * xf, axis=-1, keepdims=True))
    rinv = lax.rsqrt(ms + 1e-05)
    normed = (xf * rinv * g).astype(jnp.bfloat16)
    pre = jnp.dot(normed, down, preferred_element_type=jnp.float32)
    sig = jax.nn.sigmoid(pre)
    act = (pre * sig).astype(jnp.bfloat16)
    out = (xf + jnp.dot(act, up, preferred_element_type=jnp.float32)).astype(jnp.bfloat16)
    dact = lax.dot_general(dy, up, (((1,), (1,)), ((), ())), preferred_element_type=jnp.float32)
    dpre = (dact * sig * (1.0 + pre * (1.0 - sig))).astype(jnp.bfloat16)
    gup = lax.dot_general(act, dy, (((0,), (0,)), ((), ())), preferred_element_type=jnp.float32).astype(jnp.bfloat16)
    gdown = lax.dot_general(normed, dpre, (((0,), (0,)), ((), ())), preferred_element_type=jnp.float32).astype(jnp.bfloat16)
    dnorm = lax.dot_general(dpre, down, (((1,), (1,)), ((), ())), preferred_element_type=jnp.float32) * g
    inner = lax.optimization_barrier(jnp.mean(dnorm * xf, axis=-1, keepdims=True))
    dx = (dy.astype(jnp.float32) + rinv * (dnorm - xf * rinv * rinv * inner)).astype(jnp.bfloat16)
    return (out, dx, gdown, gup)

def destinations(counts):
    cum = jnp.cumsum(counts, axis=1)
    start = cum - counts
    colstart = jnp.cumsum(counts, axis=0) - counts
    blocks = jnp.arange(NB, dtype=jnp.int32)
    target = lax.optimization_barrier(jnp.sum((cum[:, None, :] <= blocks[None, :, None]).astype(jnp.int32), axis=2)).astype(jnp.int32)
    first = jnp.take_along_axis(start, target, axis=1)
    offset = jnp.take_along_axis(colstart, target, axis=1)
    dest = target * NB + offset + blocks[None, :] - first
    return dest.reshape(-1).astype(jnp.int32)

def reference(inputs, out_grad, gains, down_proj, up_proj, wiring, pair_mask):
    flat_x = inputs.reshape(SECTIONS * PEERS, TOK, D)
    flat_dy = out_grad.reshape(SECTIONS * PEERS, TOK, D)

    def single(index):
        section = index // PEERS
        return layer(flat_x[index], flat_dy[index], gains[section], down_proj[section], up_proj[section])
    outs, dxs, gdowns, gups = lax.map(single, jnp.arange(SECTIONS * PEERS, dtype=jnp.int32))
    out_blocks = outs.reshape(SECTIONS, PEERS * NB, BLK, D)
    dx_blocks = dxs.reshape(SECTIONS, PEERS * NB, BLK, D)
    dest = jax.vmap(destinations)(wiring)

    def place(where, blocks):
        return jnp.zeros_like(blocks).at[where].set(blocks)
    routed = jax.vmap(place)(dest, out_blocks)
    next_inputs = jnp.roll(routed, 1, axis=0).reshape(SECTIONS, PEERS, TOK, D)
    later = jnp.roll(dx_blocks, -1, axis=0)
    returned = jax.vmap(lambda where, blocks: blocks[where])(dest, later)
    returned_grad = returned.reshape(SECTIONS, PEERS, TOK, D)
    partner = jnp.bitwise_xor(jnp.arange(PEERS, dtype=jnp.int32)[None, :], pair_mask[:, None])
    gd = gdowns.reshape(SECTIONS, PEERS, D, R).astype(jnp.float32)
    gu = gups.reshape(SECTIONS, PEERS, R, D).astype(jnp.float32)
    gd_other = jnp.take_along_axis(gd, partner[:, :, None, None], axis=1)
    gu_other = jnp.take_along_axis(gu, partner[:, :, None, None], axis=1)
    return (next_inputs, returned_grad, (gd + gd_other) * 0.5, (gu + gu_other) * 0.5)
```

```python
import functools

import jax
import jax.numpy as jnp
from jax import lax
from jax.experimental import pallas as pl
from jax.experimental.pallas import tpu as pltpu
from jax.sharding import PartitionSpec as P

CAP = 2
TILE = 512
CHUNKS = (2, 2, 2, 3, 1)
STAGES = (((0, 1, 2), (0, 1)), ((3, 4), (2, 3)), ((), (4,)))
F32, BF16 = jnp.float32, jnp.bfloat16


def passed_along(block, axis, distance):
    devices = range(lax.axis_size(axis))
    route = [((i - distance) % len(devices), i) for i in devices]
    return lax.ppermute(block, axis, route)


def swapped(block, axis, mask):
    count = lax.axis_size(axis)
    return lax.ppermute(block, axis, [(i, i ^ mask) for i in range(count) if i ^ mask < count])


def dot(a, b, dims):
    return lax.dot_general(a, b, (dims, ((), ())), preferred_element_type=F32)


def plan_kernel(place_ref, wiring_ref, mask_ref, plan_ref):
    section, peer = place_ref[0], place_ref[1]
    count = wiring_ref.shape[0]
    before = lax.rem(section + count - 1, count)
    mask = mask_ref[section]
    match = peer ^ mask
    other = peer ^ jnp.where(mask >= 2, 1, 2)

    def sources(back, q):
        at = [jnp.int32(0)] * 4
        block = [jnp.int32(0)] * 4
        cum = jnp.int32(0)
        for i in range(4):
            first = jnp.int32(0)
            for j in range(4):
                if back:
                    first += jnp.where(j < q, wiring_ref[before, j, i], 0)
                else:
                    first += jnp.where(j < q, wiring_ref[section, i, j], 0)
            amount = wiring_ref[before, q, i] if back else wiring_ref[section, i, q]
            for k in range(4):
                inside = (cum <= k) & (k < cum + amount)
                at[k] = jnp.where(inside, i, at[k])
                block[k] = jnp.where(inside, first + k - cum, block[k])
            cum += amount
        held = [((a == peer) | (a == match)).astype(jnp.int32) for a in at]
        index = [jnp.where(a == peer, b, 4 + b) for a, b in zip(at, block)]
        return held, index

    for n, back in enumerate((False, True)):
        held, index = sources(back, other)
        rank = jnp.int32(0)
        ranks = []
        for k in range(4):
            ranks.append(rank)
            rank += held[k]
        for j in range(4):
            pick = jnp.int32(0)
            for k in range(4):
                pick += jnp.where((held[k] == 1) & (ranks[k] == j), index[k], 0)
            plan_ref[4 * n + j] = pick
        held, index = sources(back, peer)
        rank = jnp.int32(0)
        for k in range(4):
            plan_ref[8 + 4 * n + k] = jnp.where(held[k] == 1, index[k], 8 + rank)
            rank += 1 - held[k]


def make_plan(place, wiring, pair_mask):
    smem = pl.BlockSpec(memory_space=pltpu.SMEM)
    return pl.pallas_call(
        plan_kernel,
        out_shape=jax.ShapeDtypeStruct((16,), jnp.int32),
        in_specs=[smem] * 3,
        out_specs=smem,
        name="plan",
    )(place, wiring, pair_mask)


def rows_kernel(cap, blk, plan_ref, x_ref, dy_ref, got_ref, act_ref, dpre_ref, stat_ref, up_ref, down_ref, g_ref,
                send_ref, keep_f_ref, keep_b_ref, out_scr, dx_scr):
    rows = x_ref.shape[0]
    for half in range(2):
        part = pl.ds(half * rows, rows)
        x = (x_ref[...] if half == 0 else got_ref[:rows, :]).astype(F32)
        dy = (dy_ref[...] if half == 0 else got_ref[rows:, :]).astype(F32)
        out = x + dot(act_ref[part, :], up_ref[...], ((1,), (0,)))
        out_scr[part, :] = out.astype(BF16)
        dn = dot(dpre_ref[part, :], down_ref[...], ((1,), (1,))) * g_ref[...]
        dx = dy + stat_ref[part, 0:1] * dn - x * stat_ref[part, 1:2]
        dx_scr[part, :] = dx.astype(BF16)

    def block_of(scr, index):
        return scr[pl.ds(pl.multiple_of(index * blk, blk), blk), :]

    for n, scr in enumerate((out_scr, dx_scr)):
        for j in range(cap):
            send_ref[pl.ds((n * cap + j) * blk, blk), :] = block_of(scr, plan_ref[4 * n + j])
    for n, (scr, keep_ref) in enumerate(((out_scr, keep_f_ref), (dx_scr, keep_b_ref))):
        for k in range(4):
            keep_ref[pl.ds(k * blk, blk), :] = block_of(scr, jnp.minimum(plan_ref[8 + 4 * n + k], 7))


def make_rows(cap, first, tiles, plan, x, dy, got, act, dpre, stat, up, down, g):
    rows, width = x.shape
    rank = up.shape[0]
    blk = rows // 4
    whole = lambda shape: pl.BlockSpec(shape, lambda i: (0, 0))
    here = lambda n: pl.BlockSpec((n, TILE), lambda i: (0, i))
    there = lambda n: pl.BlockSpec((n, TILE), lambda i: (0, first + i))
    cols = tiles * TILE
    return pl.pallas_call(
        functools.partial(rows_kernel, cap, blk),
        grid=(tiles,),
        out_shape=(
            jax.ShapeDtypeStruct((2 * cap * blk, cols), BF16),
            jax.ShapeDtypeStruct((rows, cols), BF16),
            jax.ShapeDtypeStruct((rows, cols), BF16),
        ),
        in_specs=[
            pl.BlockSpec(memory_space=pltpu.SMEM),
            there(rows), there(rows), here(2 * rows),
            whole((2 * rows, rank)), whole((2 * rows, rank)), whole((2 * rows, 2)),
            there(rank), pl.BlockSpec((TILE, rank), lambda i: (first + i, 0)), there(1),
        ],
        out_specs=(here(2 * cap * blk), here(rows), here(rows)),
        scratch_shapes=[pltpu.VMEM((2 * rows, TILE), BF16), pltpu.VMEM((2 * rows, TILE), BF16)],
        compiler_params=pltpu.CompilerParams(vmem_limit_bytes=32 * 2**20),
        cost_estimate=pl.CostEstimate(flops=8 * rows * rank * cols, bytes_accessed=20 * rows * cols, transcendentals=0),
        name="rows",
    )(plan, x, dy, got, act, dpre, stat, up, down, g)


def merge_kernel(cap, blk, plan_ref, keep_f_ref, keep_b_ref, got_ref, f_ref, b_ref):
    for n, (keep_ref, to_ref) in enumerate(((keep_f_ref, f_ref), (keep_b_ref, b_ref))):
        for k in range(4):
            index = plan_ref[8 + 4 * n + k]
            at = pl.ds(k * blk, blk)

            @pl.when(index < 8)
            def _():
                to_ref[at, :] = keep_ref[at, :]

            @pl.when(index >= 8)
            def _():
                row = (n * cap + jnp.clip(index - 8, 0, cap - 1)) * blk
                to_ref[at, :] = got_ref[pl.ds(pl.multiple_of(row, blk), blk), :]


def make_merge(cap, plan, keep_f, keep_b, got):
    rows, cols = keep_f.shape
    blk = rows // 4
    here = lambda n: pl.BlockSpec((n, TILE), lambda i: (0, i))
    return pl.pallas_call(
        functools.partial(merge_kernel, cap, blk),
        grid=(cols // TILE,),
        out_shape=(jax.ShapeDtypeStruct((rows, cols), BF16),) * 2,
        in_specs=[pl.BlockSpec(memory_space=pltpu.SMEM), here(rows), here(rows), here(2 * cap * blk)],
        out_specs=(here(rows), here(rows)),
        compiler_params=pltpu.CompilerParams(vmem_limit_bytes=32 * 2**20),
        cost_estimate=pl.CostEstimate(flops=0, bytes_accessed=12 * rows * cols, transcendentals=0),
        name="merge",
    )(plan, keep_f, keep_b, got)


def grads_kernel(starts, x_ref, dy_ref, *refs):
    got_refs = refs[: len(starts) - 1]
    act_ref, dpre_ref, stat_ref, g_ref, gup_ref, gdown_ref, x_scr, dy_scr = refs[len(starts) - 1 :]
    step = pl.program_id(0)
    rows = x_ref.shape[0]
    dy_scr[:rows, :] = dy_ref[...]
    x_scr[:rows, :] = x_ref[...]
    for c, got_ref in enumerate(got_refs):

        @pl.when((step >= starts[c]) & (step < starts[c + 1]))
        def _():
            x_scr[rows:, :] = got_ref[:rows, :]
            dy_scr[rows:, :] = got_ref[rows:, :]

    gup_ref[...] = dot(act_ref[...], dy_scr[...], ((0,), (0,))) * 0.5
    normed = (x_scr[...].astype(F32) * stat_ref[:, 0:1] * g_ref[...]).astype(BF16)
    gdown_ref[...] = dot(normed, dpre_ref[...], ((0,), (0,))) * 0.5


def make_grads(x, dy, got, act, dpre, stat, g):
    rows, width = x.shape
    rank = act.shape[1]
    starts = [0]
    for block in got:
        starts.append(starts[-1] + block.shape[1] // TILE)

    def chunk(c):
        low, high = starts[c], starts[c + 1]
        return pl.BlockSpec((2 * rows, TILE), lambda i: (0, jnp.clip(i - low, 0, high - low - 1)))

    whole = lambda shape: pl.BlockSpec(shape, lambda i: (0, 0))
    here = lambda n: pl.BlockSpec((n, TILE), lambda i: (0, i))
    return pl.pallas_call(
        functools.partial(grads_kernel, tuple(starts)),
        grid=(width // TILE,),
        out_shape=(jax.ShapeDtypeStruct((rank, width), F32), jax.ShapeDtypeStruct((width, rank), F32)),
        in_specs=[here(rows), here(rows)] + [chunk(c) for c in range(len(got))]
        + [whole((2 * rows, rank)), whole((2 * rows, rank)), whole((2 * rows, 2)), here(1)],
        out_specs=(here(rank), pl.BlockSpec((TILE, rank), lambda i: (i, 0))),
        scratch_shapes=[pltpu.VMEM((2 * rows, TILE), BF16), pltpu.VMEM((2 * rows, TILE), BF16)],
        compiler_params=pltpu.CompilerParams(vmem_limit_bytes=32 * 2**20),
        cost_estimate=pl.CostEstimate(flops=8 * rows * rank * width, bytes_accessed=16 * rows * width, transcendentals=0),
        name="grads",
    )(x, dy, *got, act, dpre, stat, g)


def adapter(x, dy, g, down, up):
    xf = x.astype(F32)
    rinv = lax.rsqrt(jnp.mean(xf * xf, axis=-1, keepdims=True) + 1e-05)
    normed = (xf * rinv * g).astype(BF16)
    pre = dot(normed, down, ((1,), (0,)))
    sig = jax.nn.sigmoid(pre)
    act = (pre * sig).astype(BF16)
    dact = dot(dy, up, ((1,), (1,)))
    dpre = (dact * sig * (1.0 + pre * (1.0 - sig))).astype(BF16)
    inner = jnp.sum(dpre.astype(F32) * pre, axis=-1, keepdims=True) / x.shape[1]
    return act, dpre, rinv, rinv * rinv * inner


def four_peers(inputs, out_grad, gains, down_proj, up_proj, wiring, pair_mask):
    sections = lax.axis_size("section")
    section = lax.axis_index("section")
    peer = lax.axis_index("peer")
    x, dy, down, up = inputs[0, 0], out_grad[0, 0], down_proj[0], up_proj[0]
    rows, width = x.shape
    starts = [sum(CHUNKS[:c]) for c in range(len(CHUNKS) + 1)]
    mask = pair_mask[section]
    wide = (jnp.sum((wiring == 2).astype(jnp.int32)) > sections * 4).astype(jnp.int32)
    choice = mask - 1 + 3 * wide
    place = jnp.stack([section, peer]).astype(jnp.int32)

    def outgoing(c):
        cols = slice(starts[c] * TILE, starts[c + 1] * TILE)
        return jnp.concatenate([x[:, cols], dy[:, cols]], axis=0)

    def stage(number, cap, mask, carry):
        exchange, route = STAGES[number]
        other = 1 if mask >= 2 else 2
        got = {}
        if number == 0:
            got[0] = swapped(outgoing(0), "peer", mask)
            plan = make_plan(place, wiring, pair_mask)
            act, dpre, rinv, weight = adapter(x, dy, gains, down, up)
            low = jnp.concatenate([act, dpre], axis=0)
            high = jnp.concatenate([rinv.reshape(1, rows), weight.reshape(1, rows)], axis=0)
            low2, high2 = swapped((low, high), "peer", mask)
            act2 = jnp.concatenate([act, low2[:rows]], axis=0)
            dpre2 = jnp.concatenate([dpre, low2[rows:]], axis=0)
            stat2 = jnp.concatenate([high, high2], axis=1).T
            held = {}
        else:
            plan, act2, dpre2, stat2, held = carry
        for c in exchange:
            if c not in got:
                got[c] = swapped(outgoing(c), "peer", mask)
        held = {**held, **got}
        fs, bs = [], []
        for c in route:
            send, keep_f, keep_b = make_rows(
                cap, starts[c], CHUNKS[c], plan, x, dy, held[c], act2, dpre2, stat2, up, down, gains
            )
            back = swapped(send, "peer", other)
            f, b = make_merge(cap, plan, keep_f, keep_b, back)
            fs.append(f)
            bs.append(b)
        f = jnp.concatenate(fs, axis=1) if len(fs) > 1 else fs[0]
        b = jnp.concatenate(bs, axis=1) if len(bs) > 1 else bs[0]
        common = (plan, act2, dpre2, stat2) if number == 0 else None
        return f, b, got, common

    carry, held = None, {}
    nexts, returns = [], []
    for number in range(len(STAGES)):
        branches = [functools.partial(stage, number, cap, m) for cap in (3, 4) for m in (1, 2, 3)]
        f, b, got, common = lax.switch(choice, branches, carry if number == 0 else (*keep, held))
        if number == 0:
            keep = common
        held = {**held, **got}
        nexts.append(passed_along(f, "section", 1))
        returns.append(passed_along(b, "section", -1))
    grad_up, grad_down = make_grads(x, dy, [held[c] for c in range(len(CHUNKS))], *keep[1:], gains)
    next_rows = jnp.concatenate(nexts, axis=1)
    return_rows = jnp.concatenate(returns, axis=1)
    return next_rows[None, None], return_rows[None, None], grad_down[None, None], grad_up[None, None]


def layer(x, dy, g, down, up):
    xf = x.astype(F32)
    act, dpre, rinv, weight = adapter(x, dy, g, down, up)
    normed = (xf * rinv * g).astype(BF16)
    out = (xf + dot(act, up, ((1,), (0,)))).astype(BF16)
    gup = dot(act, dy, ((0,), (0,))).astype(BF16)
    gdown = dot(normed, dpre, ((0,), (0,))).astype(BF16)
    dnorm = dot(dpre, down, ((1,), (1,))) * g
    dx = (dy.astype(F32) + rinv * dnorm - xf * weight).astype(BF16)
    return (out, dx, gdown, gup)


def pack_blocks(blocks, counts_vec, first_vec, slots):
    peers = counts_vec.shape[0]
    nblocks = blocks.shape[0]
    place = jnp.arange(slots, dtype=jnp.int32)
    source = first_vec[:, None] + place[None, :]
    valid = place[None, :] < counts_vec[:, None]
    select = (source[:, :, None] == jnp.arange(nblocks, dtype=jnp.int32)[None, None, :]) & valid[:, :, None]
    select = select.astype(BF16).reshape(peers * slots, nblocks)
    return jnp.dot(select, blocks, preferred_element_type=F32).astype(BF16)


def unpack_blocks(received, counts_vec, first_vec, slots, nblocks):
    place = jnp.arange(slots, dtype=jnp.int32)
    target = (first_vec[:, None] + place[None, :]).reshape(-1)
    valid = (place[None, :] < counts_vec[:, None]).reshape(-1)
    select = (target[None, :] == jnp.arange(nblocks, dtype=jnp.int32)[:, None]) & valid[None, :]
    return jnp.dot(select.astype(BF16), received, preferred_element_type=F32).astype(BF16)


def any_peers(inputs, out_grad, gains, down_proj, up_proj, wiring, pair_mask):
    sections = lax.axis_size("section")
    nblocks = lax.axis_size("peer")
    section = lax.axis_index("section")
    peer = lax.axis_index("peer")
    x = inputs[0, 0]
    rows, width = x.shape
    out, dx, gdown, gup = layer(x, out_grad[0, 0], gains[0], down_proj[0], up_proj[0])
    blk_rows = rows // nblocks
    here = lax.dynamic_index_in_dim(wiring, section, 0, keepdims=False)
    before = lax.dynamic_index_in_dim(wiring, (section + sections - 1) % sections, 0, keepdims=False)
    here_start = jnp.cumsum(here, axis=1) - here
    before_col = jnp.cumsum(before, axis=0) - before
    out_blocks = out.reshape(nblocks, blk_rows * width)
    dx_blocks = dx.reshape(nblocks, blk_rows * width)
    fwd_buf = pack_blocks(out_blocks, here[peer], here_start[peer], CAP)
    back_buf = pack_blocks(dx_blocks, before[:, peer], before_col[:, peer], CAP)
    moved = passed_along(fwd_buf, "section", 1)
    got_fwd = lax.all_to_all(moved, "peer", split_axis=0, concat_axis=0, tiled=True)
    next_rows = unpack_blocks(got_fwd, before[:, peer], before_col[:, peer], CAP, nblocks)
    moved_back = passed_along(back_buf, "section", -1)
    got_back = lax.all_to_all(moved_back, "peer", split_axis=0, concat_axis=0, tiled=True)
    return_rows = unpack_blocks(got_back, here[peer], here_start[peer], CAP, nblocks)
    mask_value = pair_mask[section]
    other_down, other_up = (gdown, gup)
    for bit in range(nblocks.bit_length() - 1):
        swapped_down, swapped_up = swapped((other_down, other_up), "peer", 1 << bit)
        take = jnp.bitwise_and(jnp.right_shift(mask_value, bit), 1) == 1
        other_down = jnp.where(take, swapped_down, other_down)
        other_up = jnp.where(take, swapped_up, other_up)
    grad_down = (gdown.astype(F32) + other_down.astype(F32)) * 0.5
    grad_up = (gup.astype(F32) + other_up.astype(F32)) * 0.5
    return (
        next_rows.reshape(1, 1, rows, width),
        return_rows.reshape(1, 1, rows, width),
        grad_down[None, None],
        grad_up[None, None],
    )


def solution(mesh):
    whole = P("section", "peer", None, None)
    return jax.shard_map(
        four_peers if mesh.shape["peer"] == 4 else any_peers,
        mesh=mesh,
        in_specs=(whole, whole, P("section", None), P("section", None, None), P("section", None, None), P(), P()),
        out_specs=(whole,) * 4,
        check_vma=False,
    )
```

```python
import functools

import jax
import jax.numpy as jnp
from jax import lax
from jax.experimental import pallas as pl
from jax.experimental.pallas import tpu as pltpu
from jax.sharding import PartitionSpec as P

CAP = 2
TILE = 512
CHUNKS = (2, 2, 2, 2, 2)
STAGES = (((0, 1, 2), (0, 1)), ((3, 4), (2, 3)), ((), (4,)))
DEPTH = 1
F32, BF16 = jnp.float32, jnp.bfloat16


def passed_along(block, axis, distance):
    devices = range(lax.axis_size(axis))
    route = [((i - distance) % len(devices), i) for i in devices]
    return lax.ppermute(block, axis, route)


def swapped(block, axis, mask):
    count = lax.axis_size(axis)
    return lax.ppermute(block, axis, [(i, i ^ mask) for i in range(count) if i ^ mask < count])


def after(value, *others):
    return lax.optimization_barrier((value, *others))[0]


def dot(a, b, dims):
    return lax.dot_general(a, b, (dims, ((), ())), preferred_element_type=F32)


PIECE = 1024
FREE = pl.CostEstimate(flops=0, bytes_accessed=0, transcendentals=0)
ROOM = pltpu.CompilerParams(vmem_limit_bytes=32 * 2**20)
SMEM = pl.BlockSpec(memory_space=pltpu.SMEM)


def open_kernel(widths, wiring_ref, mask_ref, g_ref, x_ref, dy_ref, down_ref, up_ref, plan_ref, choice_ref, low_ref,
                high_ref, *refs):
    outs = refs[: len(widths)]
    x_scr, dy_scr, down_scr, up_scr, extra, in_sems, out_sems, extra_sem = refs[len(widths) :]
    rows, width = x_ref.shape
    rank = up_ref.shape[0]
    pieces = [slice(i, i + PIECE) for i in range(0, width, PIECE)]
    loads = []
    for i, at in enumerate(pieces):
        pairs = ((x_ref.at[:, at], x_scr.at[:, at]), (dy_ref.at[:, at], dy_scr.at[:, at]),
                 (down_ref.at[at, :], down_scr.at[at, :]), (up_ref.at[:, at], up_scr.at[:, at]))
        loads.append([pltpu.make_async_copy(s, t, in_sems.at[4 * i + n]) for n, (s, t) in enumerate(pairs)])
    for some in loads:
        for copy in some:
            copy.start()
    stores, first = [], 0
    for c, cols in enumerate(widths):
        for n, scr in enumerate((x_scr, dy_scr)):
            to = outs[c].at[pl.ds(n * rows, rows), :]
            stores.append((first + cols, pltpu.make_async_copy(scr.at[:, pl.ds(first, cols)], to, out_sems.at[2 * c + n])))
        first += cols

    section, peer = lax.axis_index("section"), lax.axis_index("peer")
    count = wiring_ref.shape[0]
    before = lax.rem(section + count - 1, count)
    mask = mask_ref[section]
    match = peer ^ mask
    other = peer ^ jnp.where(mask >= 2, 1, 2)

    def sources(back, q):
        at = [jnp.int32(0)] * 4
        block = [jnp.int32(0)] * 4
        cum = jnp.int32(0)
        for i in range(4):
            first = jnp.int32(0)
            for j in range(4):
                if back:
                    first += jnp.where(j < q, wiring_ref[before, j, i], 0)
                else:
                    first += jnp.where(j < q, wiring_ref[section, i, j], 0)
            amount = wiring_ref[before, q, i] if back else wiring_ref[section, i, q]
            for k in range(4):
                inside = (cum <= k) & (k < cum + amount)
                at[k] = jnp.where(inside, i, at[k])
                block[k] = jnp.where(inside, first + k - cum, block[k])
            cum += amount
        held = [((a == peer) | (a == match)).astype(jnp.int32) for a in at]
        index = [jnp.where(a == peer, b, 4 + b) for a, b in zip(at, block)]
        return held, index

    for n, back in enumerate((False, True)):
        held, index = sources(back, other)
        order = jnp.int32(0)
        orders = []
        for k in range(4):
            orders.append(order)
            order += held[k]
        for j in range(4):
            pick = jnp.int32(0)
            for k in range(4):
                pick += jnp.where((held[k] == 1) & (orders[k] == j), index[k], 0)
            plan_ref[4 * n + j] = pick
        held, index = sources(back, peer)
        order = jnp.int32(0)
        for k in range(4):
            plan_ref[8 + 4 * n + k] = jnp.where(held[k] == 1, index[k], 8 + order)
            order += 1 - held[k]
    twos = jnp.int32(0)
    for at in (section, before):
        for i in range(4):
            for j in range(4):
                twos += jnp.where(wiring_ref[at, i, j] == 2, 1, 0)
    choice_ref[0] = mask - 1 + jnp.where(twos > 8, 3, 0)

    square = jnp.zeros((rows, 1), F32)
    pre = jnp.zeros((rows, rank), F32)
    dact = jnp.zeros((rows, rank), F32)
    for some, at in zip(loads, pieces):
        for copy in some:
            copy.wait()
        for end, copy in stores:
            if at.start < end <= at.stop:
                copy.start()
        x = x_scr[:, at].astype(F32)
        square += jnp.sum(x * x, axis=1, keepdims=True)
        pre += dot((x * g_ref[:, at]).astype(BF16), down_scr[at, :], ((1,), (0,)))
        dact += dot(dy_scr[:, at], up_scr[:, at], ((1,), (1,)))
    rinv = lax.rsqrt(square / width + 1e-05)
    v = pre * rinv
    sig = jax.nn.sigmoid(v)
    act = (v * sig).astype(BF16)
    dpre = (dact * sig * (1.0 + v * (1.0 - sig))).astype(BF16)
    inner = jnp.sum(dpre.astype(F32) * v, axis=1, keepdims=True) / width
    weight = rinv * rinv * inner
    low_ref[:rows, :] = act
    low_ref[rows:, :] = dpre
    lane = lax.broadcasted_iota(jnp.int32, (rows, rows), 1)
    high = jnp.where(lane == 0, rinv, weight).T[:8, :]
    high_ref[...] = high
    bands = widths[0] // rank
    band = 2 * rows // bands
    for j in range(bands):
        from_ref = act if (j + 1) * band <= rows else dpre
        start = j * band % rows
        extra[:band, j * rank : (j + 1) * rank] = from_ref[start : start + band, :]
    rest = high
    parts = []
    for _ in range(3):
        part = rest.astype(BF16)
        parts.append(part)
        rest = rest - part.astype(F32)
    extra[band:, :] = jnp.zeros_like(extra[band:, :])
    extra[band : band + 16, 0:rows] = jnp.concatenate([parts[0], parts[1]], axis=0)
    extra[band : band + 16, rows : 2 * rows] = jnp.concatenate([parts[2], parts[2]], axis=0)
    last = pltpu.make_async_copy(extra, outs[0].at[pl.ds(2 * rows, band + 16), :], extra_sem)
    last.start()
    for _, copy in stores:
        copy.wait()
    last.wait()


def make_open(widths, wiring, pair_mask, g, x, dy, down, up):
    rows, width = x.shape
    rank = up.shape[0]
    band = 2 * rows * rank // widths[0]
    hbm = pl.BlockSpec(memory_space=pl.ANY)
    vmem = pl.BlockSpec(memory_space=pltpu.VMEM)
    tall = [2 * rows + band + 16] + [2 * rows] * (len(widths) - 1)
    return pl.pallas_call(
        functools.partial(open_kernel, widths),
        out_shape=[
            jax.ShapeDtypeStruct((16,), jnp.int32),
            jax.ShapeDtypeStruct((1,), jnp.int32),
            jax.ShapeDtypeStruct((2 * rows, rank), BF16),
            jax.ShapeDtypeStruct((8, rows), F32),
        ] + [jax.ShapeDtypeStruct((n, cols), BF16) for n, cols in zip(tall, widths)],
        in_specs=[SMEM, SMEM, vmem, hbm, hbm, hbm, hbm],
        out_specs=[SMEM, SMEM, vmem, vmem] + [hbm] * len(widths),
        scratch_shapes=[
            pltpu.VMEM((rows, width), BF16), pltpu.VMEM((rows, width), BF16),
            pltpu.VMEM((width, rank), BF16), pltpu.VMEM((rank, width), BF16),
            pltpu.VMEM((band + 16, widths[0]), BF16),
            pltpu.SemaphoreType.DMA((4 * (width // PIECE),)), pltpu.SemaphoreType.DMA((2 * len(widths),)),
            pltpu.SemaphoreType.DMA,
        ],
        compiler_params=ROOM,
        cost_estimate=FREE,
        name="open",
    )(wiring, pair_mask, g, x, dy, down, up)


def unpack_kernel(got_ref, low_ref, high_ref):
    rows2, rank = low_ref.shape
    bands = got_ref.shape[1] // rank
    band = rows2 // bands
    rows = rows2 // 2
    for j in range(bands):
        low_ref[j * band : (j + 1) * band, :] = got_ref[rows2 : rows2 + band, j * rank : (j + 1) * rank]
    parts = got_ref[rows2 + band : rows2 + band + 16, :].astype(F32)
    high_ref[...] = parts[0:8, 0:rows] + parts[8:16, 0:rows] + parts[0:8, rows : 2 * rows]


def make_unpack(got, low, high):
    vmem = pl.BlockSpec(memory_space=pltpu.VMEM)
    return pl.pallas_call(
        unpack_kernel,
        out_shape=(jax.ShapeDtypeStruct(low.shape, BF16), jax.ShapeDtypeStruct(high.shape, F32)),
        in_specs=[vmem],
        out_specs=(vmem, vmem),
        compiler_params=ROOM,
        cost_estimate=FREE,
        name="unpack",
    )(got)


def whole(shape):
    return pl.BlockSpec(shape, lambda i: (0,) * len(shape))


def column(rows, first=0):
    return pl.BlockSpec((rows, TILE), lambda i: (0, first + i))


def chunk(rows, start, end):
    return pl.BlockSpec((rows, TILE), lambda i: (0, jnp.clip(i - start, 0, end - start - 1)))


def rows_kernel(cap, blk, plan_ref, x_ref, dy_ref, got_ref, low_ref, low2_ref, high_ref, high2_ref, up_ref, down_ref,
                g_ref, send_ref, keep_f_ref, keep_b_ref, out_scr, dx_scr):
    rows = x_ref.shape[0]
    for half in range(2):
        part = pl.ds(half * rows, rows)
        x = (x_ref[...] if half == 0 else got_ref[:rows, :]).astype(F32)
        dy = (dy_ref[...] if half == 0 else got_ref[rows:, :]).astype(F32)
        low = low_ref if half == 0 else low2_ref
        stat = (high_ref if half == 0 else high2_ref)[...].T
        out = x + dot(low[:rows, :], up_ref[...], ((1,), (0,)))
        out_scr[part, :] = out.astype(BF16)
        dn = dot(low[rows:, :], down_ref[...], ((1,), (1,))) * g_ref[...]
        dx = dy + stat[:, 0:1] * dn - x * stat[:, 1:2]
        dx_scr[part, :] = dx.astype(BF16)

    def block_of(scr, index):
        return scr[pl.ds(pl.multiple_of(index * blk, blk), blk), :]

    for n, scr in enumerate((out_scr, dx_scr)):
        for j in range(cap):
            send_ref[pl.ds((n * cap + j) * blk, blk), :] = block_of(scr, plan_ref[4 * n + j])
    for n, (scr, keep_ref) in enumerate(((out_scr, keep_f_ref), (dx_scr, keep_b_ref))):
        for k in range(4):
            keep_ref[pl.ds(k * blk, blk), :] = block_of(scr, jnp.minimum(plan_ref[8 + 4 * n + k], 7))


def make_rows(cap, first, tiles, plan, x, dy, got, low, low2, high, high2, up, down, g):
    rows, width = x.shape
    rank = up.shape[0]
    blk = rows // 4
    cols = tiles * TILE
    return pl.pallas_call(
        functools.partial(rows_kernel, cap, blk),
        grid=(tiles,),
        out_shape=(
            jax.ShapeDtypeStruct((2 * cap * blk, cols), BF16),
            jax.ShapeDtypeStruct((rows, cols), BF16),
            jax.ShapeDtypeStruct((rows, cols), BF16),
        ),
        in_specs=[
            SMEM, column(rows, first), column(rows, first), column(2 * rows),
            whole(low.shape), whole(low.shape), whole(high.shape), whole(high.shape),
            column(rank, first), pl.BlockSpec((TILE, rank), lambda i: (first + i, 0)), column(1, first),
        ],
        out_specs=(column(2 * cap * blk), column(rows), column(rows)),
        scratch_shapes=[pltpu.VMEM((2 * rows, TILE), BF16), pltpu.VMEM((2 * rows, TILE), BF16)],
        compiler_params=ROOM,
        cost_estimate=FREE,
        name="rows",
    )(plan, x, dy, got, low, low2, high, high2, up, down, g)


def merge_kernel(cap, blk, spans, plan_ref, *refs):
    outs, sems = refs[-3:-1], refs[-1]
    waits = []
    for c, (first, cols) in enumerate(spans):
        keeps, got = refs[3 * c : 3 * c + 2], refs[3 * c + 2]
        for n in range(2):
            for k in range(4):
                index = plan_ref[8 + 4 * n + k]
                rows = pl.ds(k * blk, blk)
                to = outs[n].at[rows, pl.ds(first, cols)]
                sem = sems.at[8 * c + 4 * n + k]
                row = pl.multiple_of((n * cap + jnp.clip(index - 8, 0, cap - 1)) * blk, blk)
                here = pltpu.make_async_copy(keeps[n].at[rows, :], to, sem)
                there = pltpu.make_async_copy(got.at[pl.ds(row, blk), :], to, sem)

                @pl.when(index < 8)
                def _():
                    here.start()

                @pl.when(index >= 8)
                def _():
                    there.start()

                waits.append(here)
    for copy in waits:
        copy.wait()


def make_merge(cap, plan, parts):
    rows = parts[0][0].shape[0]
    spans, first = [], 0
    for keep_f, _, _ in parts:
        spans.append((first, keep_f.shape[1]))
        first += keep_f.shape[1]
    hbm = pl.BlockSpec(memory_space=pl.ANY)
    return pl.pallas_call(
        functools.partial(merge_kernel, cap, rows // 4, tuple(spans)),
        out_shape=(jax.ShapeDtypeStruct((rows, first), BF16),) * 2,
        in_specs=[SMEM] + [hbm] * (3 * len(parts)),
        out_specs=(hbm, hbm),
        scratch_shapes=[pltpu.SemaphoreType.DMA((8 * len(parts),))],
        compiler_params=ROOM,
        cost_estimate=FREE,
        name="merge",
    )(plan, *[array for part in parts for array in part])


def join_kernel(places, *refs):
    count = len(places)
    sems = refs[-1]
    outs = refs[-3:-1]
    parts = refs[-3 - 2 * count : -3]
    copies = []
    for n in range(2):
        for i, (first, cols) in enumerate(places):
            copies.append(
                pltpu.make_async_copy(parts[n * count + i], outs[n].at[:, pl.ds(first, cols)], sems.at[n * count + i])
            )
    for copy in copies:
        copy.start()
    for copy in copies:
        copy.wait()


def make_join(width, first, nexts, returns, into=()):
    rows = nexts[0].shape[0]
    places = []
    for part in nexts:
        places.append((first, part.shape[1]))
        first += part.shape[1]
    hbm = pl.BlockSpec(memory_space=pl.ANY)
    return pl.pallas_call(
        functools.partial(join_kernel, tuple(places)),
        out_shape=(jax.ShapeDtypeStruct((rows, width), BF16),) * 2,
        in_specs=[hbm] * (len(into) + 2 * len(nexts)),
        out_specs=(hbm, hbm),
        scratch_shapes=[pltpu.SemaphoreType.DMA((2 * len(nexts),))],
        input_output_aliases={i: i for i in range(len(into))},
        compiler_params=ROOM,
        cost_estimate=FREE,
        name="join",
    )(*into, *nexts, *returns)


def grads_kernel(starts, x_ref, dy_ref, *refs):
    got_refs = refs[: len(starts) - 1]
    low_ref, low2_ref, high_ref, high2_ref, g_ref = refs[len(starts) - 1 : len(starts) + 4]
    gup_ref, gdown_ref, x_scr, dy_scr, act_scr, dpre_scr, rinv_scr = refs[-7:]
    step = pl.program_id(0)
    rows = x_ref.shape[0]

    @pl.when(step == 0)
    def _():
        for half, (low, high) in enumerate(((low_ref, high_ref), (low2_ref, high2_ref))):
            part = pl.ds(half * rows, rows)
            act_scr[part, :] = (low[:rows, :].astype(F32) * 0.5).astype(BF16)
            dpre_scr[part, :] = (low[rows:, :].astype(F32) * 0.5).astype(BF16)
            rinv_scr[part, :] = high[...].T[:, 0:1]

    dy_scr[:rows, :] = dy_ref[...]
    x_scr[:rows, :] = x_ref[...]
    for c, got_ref in enumerate(got_refs):

        @pl.when((step >= starts[c]) & (step < starts[c + 1]))
        def _():
            x_scr[rows:, :] = got_ref[:rows, :]
            dy_scr[rows:, :] = got_ref[rows:, :]

    gup_ref[...] = dot(act_scr[...], dy_scr[...], ((0,), (0,)))
    normed = (x_scr[...].astype(F32) * rinv_scr[...] * g_ref[...]).astype(BF16)
    gdown_ref[...] = dot(normed, dpre_scr[...], ((0,), (0,)))


def make_grads(first, x, dy, got, low, low2, high, high2, g, into=()):
    rows, width = x.shape
    rank = low.shape[1]
    starts = [0]
    for block in got:
        starts.append(starts[-1] + block.shape[1] // TILE)

    def kernel(*refs):
        grads_kernel(tuple(starts), *refs[len(into):])

    return pl.pallas_call(
        kernel,
        grid=(starts[-1],),
        out_shape=(jax.ShapeDtypeStruct((rank, width), F32), jax.ShapeDtypeStruct((width, rank), F32)),
        in_specs=[pl.BlockSpec(memory_space=pl.ANY)] * len(into)
        + [column(rows, first), column(rows, first)] + [chunk(2 * rows, s, e) for s, e in zip(starts[:-1], starts[1:])]
        + [whole(low.shape), whole(low.shape), whole(high.shape), whole(high.shape), column(1, first)],
        out_specs=(column(rank, first), pl.BlockSpec((TILE, rank), lambda i: (first + i, 0))),
        scratch_shapes=[
            pltpu.VMEM((2 * rows, TILE), BF16), pltpu.VMEM((2 * rows, TILE), BF16),
            pltpu.VMEM((2 * rows, rank), BF16), pltpu.VMEM((2 * rows, rank), BF16), pltpu.VMEM((2 * rows, 1), F32),
        ],
        input_output_aliases={i: i for i in range(len(into))},
        compiler_params=ROOM,
        cost_estimate=FREE,
        name="grads",
    )(*into, x, dy, *got, low, low2, high, high2, g)


def four_peers(inputs, out_grad, gains, down_proj, up_proj, wiring, pair_mask):
    x, dy, down, up = inputs[0, 0], out_grad[0, 0], down_proj[0], up_proj[0]
    width = x.shape[1]
    count = len(CHUNKS)
    early = count - 1
    starts = [sum(CHUNKS[:c]) for c in range(count + 1)]
    plan, choice, low, high, *outs = make_open(
        [n * TILE for n in CHUNKS], wiring, pair_mask, gains, x, dy, down, up
    )
    choice = choice[0]

    def stage(number, cap, mask, state):
        exchange, route = STAGES[number]
        if number == 0:
            held = {}
        else:
            low2, high2, held, grads = state
        held, parts, backs, sent = dict(held), [], {}, plan

        def send_on(c):
            ready = [source[d] for source, d in ((held, c - DEPTH), (backs, c - DEPTH - 1)) if d in source]
            held[c] = swapped(after(outs[c], *ready) if ready else outs[c], "peer", mask)

        waiting = list(exchange)
        while waiting and (waiting[0] < exchange[0] + DEPTH):
            send_on(waiting.pop(0))
        if number == 0:
            low2, high2 = make_unpack(held[0], low, high)
        common = (low, low2, high, high2)
        for c in route:
            send, keep_f, keep_b = make_rows(
                cap, starts[c], CHUNKS[c], after(plan, sent), x, dy, held[c], *common, up, down, gains
            )
            backs[c] = swapped(send, "peer", 1 if mask >= 2 else 2)
            parts.append((keep_f, keep_b, backs[c]))
            sent = send
            if waiting:
                send_on(waiting.pop(0))
        while waiting:
            send_on(waiting.pop(0))
        if number == 0:
            grads = ()
        elif number == 1:
            grads = make_grads(0, after(x, sent), dy, [held[c] for c in range(early)], *common, gains)
        merged = make_merge(cap, after(plan, sent), parts)
        return merged, (low2, high2) if number == 0 else (), {c: held[c] for c in exchange}, grads

    state = None
    nexts, returns = [], []
    for number in range(len(STAGES)):
        branches = [functools.partial(stage, number, cap, m) for cap in (3, 4) for m in (1, 2, 3)]
        (f, b), made, arrived, grads = lax.switch(choice, branches, state)
        if number == 0:
            low2, high2 = made
            held = {}
        held = {**held, **arrived}
        state = (low2, high2, held, grads)
        if number:
            f, b = after(f, nexts[-1], returns[-1]), after(b, nexts[-1], returns[-1])
        nexts.append(passed_along(f, "section", 1))
        returns.append(passed_along(b, "section", -1))
    grad_up, grad_down = make_grads(
        starts[early], after(x, f, b), dy, [held[c] for c in range(early, count)], low, low2, high, high2, gains, into=grads
    )
    joined = make_join(width, 0, [after(nexts[0], f, b), *nexts[1:-1]], returns[:-1])
    done = sum(part.shape[1] for part in nexts[:-1])
    next_rows, return_rows = make_join(width, done, nexts[-1:], returns[-1:], into=joined)
    return next_rows[None, None], return_rows[None, None], grad_down[None, None], grad_up[None, None]


def adapter(x, dy, g, down, up):
    xf = x.astype(F32)
    rinv = lax.rsqrt(jnp.mean(xf * xf, axis=-1, keepdims=True) + 1e-05)
    normed = (xf * rinv * g).astype(BF16)
    pre = dot(normed, down, ((1,), (0,)))
    sig = jax.nn.sigmoid(pre)
    act = (pre * sig).astype(BF16)
    dact = dot(dy, up, ((1,), (1,)))
    dpre = (dact * sig * (1.0 + pre * (1.0 - sig))).astype(BF16)
    inner = jnp.sum(dpre.astype(F32) * pre, axis=-1, keepdims=True) / x.shape[1]
    return act, dpre, rinv, rinv * rinv * inner


def layer(x, dy, g, down, up):
    xf = x.astype(F32)
    act, dpre, rinv, weight = adapter(x, dy, g, down, up)
    normed = (xf * rinv * g).astype(BF16)
    out = (xf + dot(act, up, ((1,), (0,)))).astype(BF16)
    gup = dot(act, dy, ((0,), (0,))).astype(BF16)
    gdown = dot(normed, dpre, ((0,), (0,))).astype(BF16)
    dnorm = dot(dpre, down, ((1,), (1,))) * g
    dx = (dy.astype(F32) + rinv * dnorm - xf * weight).astype(BF16)
    return (out, dx, gdown, gup)


def pack_blocks(blocks, counts_vec, first_vec, slots):
    peers = counts_vec.shape[0]
    nblocks = blocks.shape[0]
    place = jnp.arange(slots, dtype=jnp.int32)
    source = first_vec[:, None] + place[None, :]
    valid = place[None, :] < counts_vec[:, None]
    select = (source[:, :, None] == jnp.arange(nblocks, dtype=jnp.int32)[None, None, :]) & valid[:, :, None]
    select = select.astype(BF16).reshape(peers * slots, nblocks)
    return jnp.dot(select, blocks, preferred_element_type=F32).astype(BF16)


def unpack_blocks(received, counts_vec, first_vec, slots, nblocks):
    place = jnp.arange(slots, dtype=jnp.int32)
    target = (first_vec[:, None] + place[None, :]).reshape(-1)
    valid = (place[None, :] < counts_vec[:, None]).reshape(-1)
    select = (target[None, :] == jnp.arange(nblocks, dtype=jnp.int32)[:, None]) & valid[None, :]
    return jnp.dot(select.astype(BF16), received, preferred_element_type=F32).astype(BF16)


def any_peers(inputs, out_grad, gains, down_proj, up_proj, wiring, pair_mask):
    sections = lax.axis_size("section")
    nblocks = lax.axis_size("peer")
    section = lax.axis_index("section")
    peer = lax.axis_index("peer")
    x = inputs[0, 0]
    rows, width = x.shape
    out, dx, gdown, gup = layer(x, out_grad[0, 0], gains[0], down_proj[0], up_proj[0])
    blk_rows = rows // nblocks
    here = lax.dynamic_index_in_dim(wiring, section, 0, keepdims=False)
    before = lax.dynamic_index_in_dim(wiring, (section + sections - 1) % sections, 0, keepdims=False)
    here_start = jnp.cumsum(here, axis=1) - here
    before_col = jnp.cumsum(before, axis=0) - before
    out_blocks = out.reshape(nblocks, blk_rows * width)
    dx_blocks = dx.reshape(nblocks, blk_rows * width)
    fwd_buf = pack_blocks(out_blocks, here[peer], here_start[peer], CAP)
    back_buf = pack_blocks(dx_blocks, before[:, peer], before_col[:, peer], CAP)
    moved = passed_along(fwd_buf, "section", 1)
    got_fwd = lax.all_to_all(moved, "peer", split_axis=0, concat_axis=0, tiled=True)
    next_rows = unpack_blocks(got_fwd, before[:, peer], before_col[:, peer], CAP, nblocks)
    moved_back = passed_along(back_buf, "section", -1)
    got_back = lax.all_to_all(moved_back, "peer", split_axis=0, concat_axis=0, tiled=True)
    return_rows = unpack_blocks(got_back, here[peer], here_start[peer], CAP, nblocks)
    mask_value = pair_mask[section]
    other_down, other_up = (gdown, gup)
    for bit in range(nblocks.bit_length() - 1):
        swapped_down, swapped_up = swapped((other_down, other_up), "peer", 1 << bit)
        take = jnp.bitwise_and(jnp.right_shift(mask_value, bit), 1) == 1
        other_down = jnp.where(take, swapped_down, other_down)
        other_up = jnp.where(take, swapped_up, other_up)
    grad_down = (gdown.astype(F32) + other_down.astype(F32)) * 0.5
    grad_up = (gup.astype(F32) + other_up.astype(F32)) * 0.5
    return (
        next_rows.reshape(1, 1, rows, width),
        return_rows.reshape(1, 1, rows, width),
        grad_down[None, None],
        grad_up[None, None],
    )


def solution(mesh):
    whole = P("section", "peer", None, None)
    return jax.shard_map(
        four_peers if mesh.shape["peer"] == 4 else any_peers,
        mesh=mesh,
        in_specs=(whole, whole, P("section", None), P("section", None, None), P("section", None, None), P(), P()),
        out_specs=(whole,) * 4,
        check_vma=False,
    )
```

```python
import functools

import jax
import jax.numpy as jnp
from jax import lax
from jax.experimental import pallas as pl
from jax.experimental.pallas import tpu as pltpu
from jax.sharding import PartitionSpec as P

CAP = 2
TILE = 512
CHUNKS = (2, 2, 3, 2, 1)
STAGES = (((0, 1, 2), (0, 1)), ((3, 4), (2, 3)), ((), (4,)))
DEPTH, LAG = 2, 3
F32, BF16 = jnp.float32, jnp.bfloat16


def passed_along(block, axis, distance):
    devices = range(lax.axis_size(axis))
    route = [((i - distance) % len(devices), i) for i in devices]
    return lax.ppermute(block, axis, route)


def swapped(block, axis, mask):
    count = lax.axis_size(axis)
    return lax.ppermute(block, axis, [(i, i ^ mask) for i in range(count) if i ^ mask < count])


def after(value, *others):
    return lax.optimization_barrier((value, *others))[0]


def dot(a, b, dims):
    return lax.dot_general(a, b, (dims, ((), ())), preferred_element_type=F32)


PIECE = 1024
FREE = pl.CostEstimate(flops=0, bytes_accessed=0, transcendentals=0)
ROOM = pltpu.CompilerParams(vmem_limit_bytes=32 * 2**20)
SMEM = pl.BlockSpec(memory_space=pltpu.SMEM)


def open_kernel(widths, wiring_ref, mask_ref, g_ref, x_ref, dy_ref, down_ref, up_ref, plan_ref, choice_ref, low_ref,
                high_ref, *refs):
    outs, late_ref = refs[: len(widths)], refs[len(widths)]
    x_scr, dy_scr, down_scr, up_scr, extra, in_sems, out_sems, extra_sems = refs[len(widths) + 1 :]
    rows, width = x_ref.shape
    rank = up_ref.shape[0]
    pieces = [slice(i, i + PIECE) for i in range(0, width, PIECE)]
    loads = []
    for i, at in enumerate(pieces):
        pairs = ((x_ref.at[:, at], x_scr.at[:, at]), (dy_ref.at[:, at], dy_scr.at[:, at]),
                 (down_ref.at[at, :], down_scr.at[at, :]), (up_ref.at[:, at], up_scr.at[:, at]))
        loads.append([pltpu.make_async_copy(s, t, in_sems.at[4 * i + n]) for n, (s, t) in enumerate(pairs)])
    for some in loads:
        for copy in some:
            copy.start()
    section, peer = lax.axis_index("section"), lax.axis_index("peer")
    count = wiring_ref.shape[0]
    before = lax.rem(section + count - 1, count)
    mask = mask_ref[section]
    match = peer ^ mask
    other = peer ^ jnp.where(mask >= 2, 1, 2)

    def sources(back, q):
        at = [jnp.int32(0)] * 4
        block = [jnp.int32(0)] * 4
        cum = jnp.int32(0)
        for i in range(4):
            first = jnp.int32(0)
            for j in range(4):
                if back:
                    first += jnp.where(j < q, wiring_ref[before, j, i], 0)
                else:
                    first += jnp.where(j < q, wiring_ref[section, i, j], 0)
            amount = wiring_ref[before, q, i] if back else wiring_ref[section, i, q]
            for k in range(4):
                inside = (cum <= k) & (k < cum + amount)
                at[k] = jnp.where(inside, i, at[k])
                block[k] = jnp.where(inside, first + k - cum, block[k])
            cum += amount
        held = [((a == peer) | (a == match)).astype(jnp.int32) for a in at]
        index = [jnp.where(a == peer, b, 4 + b) for a, b in zip(at, block)]
        return held, index

    for n, back in enumerate((False, True)):
        held, index = sources(back, other)
        order = jnp.int32(0)
        orders = []
        for k in range(4):
            orders.append(order)
            order += held[k]
        for j in range(4):
            pick = jnp.int32(0)
            for k in range(4):
                pick += jnp.where((held[k] == 1) & (orders[k] == j), index[k], 0)
            plan_ref[4 * n + j] = pick
        held, index = sources(back, peer)
        order = jnp.int32(0)
        for k in range(4):
            plan_ref[8 + 4 * n + k] = jnp.where(held[k] == 1, index[k], 8 + order)
            order += 1 - held[k]
    twos = jnp.int32(0)
    for at in (section, before):
        for i in range(4):
            for j in range(4):
                twos += jnp.where(wiring_ref[at, i, j] == 2, 1, 0)
    choice_ref[0] = mask - 1 + jnp.where(twos > 8, 3, 0)
    for n, (owner, to) in enumerate(((peer, match), (match, peer))):
        wanted, cum = [jnp.int32(0)] * 4, jnp.int32(0)
        for q in range(4):
            amount = wiring_ref[before, q, owner]
            near = ((q == to) | (q == (to ^ jnp.where(mask >= 2, 1, 2)))).astype(jnp.int32)
            for k in range(4):
                wanted[k] = jnp.where((cum <= k) & (k < cum + amount), near, wanted[k])
            cum += amount
        total = sum(wanted)
        ahead, behind = jnp.int32(0), jnp.int32(0)
        slots = []
        for k in range(4):
            slots.append(jnp.where(wanted[k] == 1, ahead, total + behind))
            ahead += wanted[k]
            behind += 1 - wanted[k]
        for j in range(4):
            plan_ref[16 + 4 * n + j] = sum(jnp.where(slots[k] == j, k, 0) for k in range(4))

    blk = rows // 4
    stores, first = [], 0
    for c, cols in enumerate(widths):
        at = pl.ds(first, cols)
        first += cols
        sem = out_sems.at[4 * c]
        stores.append((first, pltpu.make_async_copy(x_scr.at[:, at], outs[c].at[pl.ds(0, rows), :], sem)))
        for j in range(3):
            from_rows = pl.ds(pl.multiple_of(plan_ref[16 + j] * blk, blk), blk)
            to = outs[c].at[pl.ds(rows + j * blk, blk), :]
            stores.append((first, pltpu.make_async_copy(dy_scr.at[from_rows, at], to, out_sems.at[4 * c + 1 + j])))
    from_rows = pl.ds(pl.multiple_of(plan_ref[19] * blk, blk), blk)
    stores.append((width, pltpu.make_async_copy(dy_scr.at[from_rows, :], late_ref, extra_sems.at[1])))

    square = jnp.zeros((rows, 1), F32)
    pre = jnp.zeros((rows, rank), F32)
    dact = jnp.zeros((rows, rank), F32)
    for some, at in zip(loads, pieces):
        for copy in some:
            copy.wait()
        for end, copy in stores:
            if at.start < end <= at.stop:
                copy.start()
        x = x_scr[:, at].astype(F32)
        square += jnp.sum(x * x, axis=1, keepdims=True)
        dact += dot(dy_scr[:, at], up_scr[:, at], ((1,), (1,)))
    rinv = lax.rsqrt(square / width + 1e-05)
    for at in pieces:
        normed = (x_scr[:, at].astype(F32) * rinv * g_ref[:, at]).astype(BF16)
        pre += dot(normed, down_scr[at, :], ((1,), (0,)))
    v = pre
    sig = jax.nn.sigmoid(v)
    act = (v * sig).astype(BF16)
    dpre = (dact * sig * (1.0 + v * (1.0 - sig))).astype(BF16)
    inner = jnp.sum(dpre.astype(F32) * v, axis=1, keepdims=True) / width
    weight = rinv * rinv * inner
    low_ref[:rows, :] = act
    low_ref[rows:, :] = dpre
    lane = lax.broadcasted_iota(jnp.int32, (rows, rows), 1)
    high = jnp.where(lane == 0, rinv, weight).T[:8, :]
    high_ref[...] = high
    bands = widths[0] // rank
    band = 2 * rows // bands
    for j in range(bands):
        from_ref = act if (j + 1) * band <= rows else dpre
        start = j * band % rows
        extra[:band, j * rank : (j + 1) * rank] = from_ref[start : start + band, :]
    rest = high
    parts = []
    for _ in range(3):
        part = rest.astype(BF16)
        parts.append(part)
        rest = rest - part.astype(F32)
    extra[band:, :] = jnp.zeros_like(extra[band:, :])
    extra[band : band + 16, 0:rows] = jnp.concatenate([parts[0], parts[1]], axis=0)
    extra[band : band + 16, rows : 2 * rows] = jnp.concatenate([parts[2], parts[2]], axis=0)
    last = pltpu.make_async_copy(extra, outs[0].at[pl.ds(rows + 3 * blk, band + 16), :], extra_sems.at[0])
    last.start()
    for _, copy in stores:
        copy.wait()
    last.wait()


def make_open(widths, wiring, pair_mask, g, x, dy, down, up):
    rows, width = x.shape
    rank = up.shape[0]
    band = 2 * rows * rank // widths[0]
    hbm = pl.BlockSpec(memory_space=pl.ANY)
    vmem = pl.BlockSpec(memory_space=pltpu.VMEM)
    sent = rows + 3 * (rows // 4)
    tall = [sent + band + 16] + [sent] * (len(widths) - 1)
    return pl.pallas_call(
        functools.partial(open_kernel, widths),
        out_shape=[
            jax.ShapeDtypeStruct((24,), jnp.int32),
            jax.ShapeDtypeStruct((1,), jnp.int32),
            jax.ShapeDtypeStruct((2 * rows, rank), BF16),
            jax.ShapeDtypeStruct((8, rows), F32),
        ] + [jax.ShapeDtypeStruct((n, cols), BF16) for n, cols in zip(tall, widths)]
        + [jax.ShapeDtypeStruct((rows // 4, width), BF16)],
        in_specs=[SMEM, SMEM, vmem, hbm, hbm, hbm, hbm],
        out_specs=[SMEM, SMEM, vmem, vmem] + [hbm] * (len(widths) + 1),
        scratch_shapes=[
            pltpu.VMEM((rows, width), BF16), pltpu.VMEM((rows, width), BF16),
            pltpu.VMEM((width, rank), BF16), pltpu.VMEM((rank, width), BF16),
            pltpu.VMEM((band + 16, widths[0]), BF16),
            pltpu.SemaphoreType.DMA((4 * (width // PIECE),)), pltpu.SemaphoreType.DMA((4 * len(widths),)),
            pltpu.SemaphoreType.DMA((2,)),
        ],
        compiler_params=ROOM,
        cost_estimate=FREE,
        name="open",
    )(wiring, pair_mask, g, x, dy, down, up)


def unpack_kernel(got_ref, low_ref, high_ref):
    rows2, rank = low_ref.shape
    bands = got_ref.shape[1] // rank
    band = rows2 // bands
    rows = rows2 // 2
    first = got_ref.shape[0] - band - 16
    for j in range(bands):
        low_ref[j * band : (j + 1) * band, :] = got_ref[first : first + band, j * rank : (j + 1) * rank]
    parts = got_ref[first + band :, :].astype(F32)
    high_ref[...] = parts[0:8, 0:rows] + parts[8:16, 0:rows] + parts[0:8, rows : 2 * rows]


def make_unpack(got, low, high):
    vmem = pl.BlockSpec(memory_space=pltpu.VMEM)
    return pl.pallas_call(
        unpack_kernel,
        out_shape=(jax.ShapeDtypeStruct(low.shape, BF16), jax.ShapeDtypeStruct(high.shape, F32)),
        in_specs=[vmem],
        out_specs=(vmem, vmem),
        compiler_params=ROOM,
        cost_estimate=FREE,
        name="unpack",
    )(got)


def whole(shape):
    return pl.BlockSpec(shape, lambda i: (0,) * len(shape))


def column(rows, first=0, tile=TILE):
    return pl.BlockSpec((rows, tile), lambda i: (0, first + i))


def chunk(rows, start, end, tile=TILE):
    return pl.BlockSpec((rows, tile), lambda i: (0, jnp.clip(i - start, 0, end - start - 1)))


def rows_kernel(cap, blk, plan_ref, x_ref, dy_ref, got_ref, low_ref, low2_ref, high_ref, high2_ref, up_ref, down_ref,
                g_ref, *refs):
    late_refs = refs[: cap - 3]
    send_ref, keep_f_ref, keep_b_ref, out_scr, dx_scr, rest_scr = refs[cap - 3 :]
    rows = x_ref.shape[0]
    for half in range(2):
        part = pl.ds(half * rows, rows)
        x = (x_ref[...] if half == 0 else got_ref[:rows, :]).astype(F32)
        low = low_ref if half == 0 else low2_ref
        stat = (high_ref if half == 0 else high2_ref)[...].T
        out = x + dot(low[:rows, :], up_ref[...], ((1,), (0,)))
        out_scr[part, :] = out.astype(BF16)
        dn = dot(low[rows:, :], down_ref[...], ((1,), (1,))) * g_ref[...]
        rest = stat[:, 0:1] * dn - x * stat[:, 1:2]
        if half == 0:
            dx_scr[part, :] = (dy_ref[...].astype(F32) + rest).astype(BF16)
        else:
            rest_scr[...] = rest
    for j in range(cap):
        dy = late_refs[0][...] if j == 3 else got_ref[rows + j * blk : rows + (j + 1) * blk, :]
        at = pl.multiple_of(plan_ref[20 + j] * blk, blk)
        dx_scr[pl.ds(rows + at, blk), :] = (dy.astype(F32) + rest_scr[pl.ds(at, blk), :]).astype(BF16)

    def block_of(scr, index):
        return scr[pl.ds(pl.multiple_of(index * blk, blk), blk), :]

    for n, scr in enumerate((out_scr, dx_scr)):
        for j in range(cap):
            send_ref[pl.ds((n * cap + j) * blk, blk), :] = block_of(scr, plan_ref[4 * n + j])
    for n, (scr, keep_ref) in enumerate(((out_scr, keep_f_ref), (dx_scr, keep_b_ref))):
        for k in range(4):
            keep_ref[pl.ds(k * blk, blk), :] = block_of(scr, jnp.minimum(plan_ref[8 + 4 * n + k], 7))


def make_rows(cap, first, tiles, plan, x, dy, got, low, low2, high, high2, up, down, g, late):
    rows, width = x.shape
    rank = up.shape[0]
    blk = rows // 4
    cols = tiles * TILE
    return pl.pallas_call(
        functools.partial(rows_kernel, cap, blk),
        grid=(tiles,),
        out_shape=(
            jax.ShapeDtypeStruct((2 * cap * blk, cols), BF16),
            jax.ShapeDtypeStruct((rows, cols), BF16),
            jax.ShapeDtypeStruct((rows, cols), BF16),
        ),
        in_specs=[
            SMEM, column(rows, first), column(rows, first), column(rows + 3 * blk),
            whole(low.shape), whole(low.shape), whole(high.shape), whole(high.shape),
            column(rank, first), pl.BlockSpec((TILE, rank), lambda i: (first + i, 0)), column(1, first),
        ] + [column(blk, first)] * (cap - 3),
        out_specs=(column(2 * cap * blk), column(rows), column(rows)),
        scratch_shapes=[
            pltpu.VMEM((2 * rows, TILE), BF16), pltpu.VMEM((2 * rows, TILE), BF16), pltpu.VMEM((rows, TILE), F32)
        ],
        compiler_params=ROOM,
        cost_estimate=FREE,
        name="rows",
    )(plan, x, dy, got, low, low2, high, high2, up, down, g, *[late] * (cap - 3))


def merge_kernel(cap, blk, spans, plan_ref, *refs):
    outs, sems = refs[-3:-1], refs[-1]
    waits = []
    for c, (first, cols) in enumerate(spans):
        keeps, got = refs[3 * c : 3 * c + 2], refs[3 * c + 2]
        for n in range(2):
            for k in range(4):
                index = plan_ref[8 + 4 * n + k]
                rows = pl.ds(k * blk, blk)
                to = outs[n].at[rows, pl.ds(first, cols)]
                sem = sems.at[8 * c + 4 * n + k]
                row = pl.multiple_of((n * cap + jnp.clip(index - 8, 0, cap - 1)) * blk, blk)
                here = pltpu.make_async_copy(keeps[n].at[rows, :], to, sem)
                there = pltpu.make_async_copy(got.at[pl.ds(row, blk), :], to, sem)

                @pl.when(index < 8)
                def _():
                    here.start()

                @pl.when(index >= 8)
                def _():
                    there.start()

                waits.append(here)
    for copy in waits:
        copy.wait()


def make_merge(cap, plan, parts):
    rows = parts[0][0].shape[0]
    spans, first = [], 0
    for keep_f, _, _ in parts:
        spans.append((first, keep_f.shape[1]))
        first += keep_f.shape[1]
    hbm = pl.BlockSpec(memory_space=pl.ANY)
    return pl.pallas_call(
        functools.partial(merge_kernel, cap, rows // 4, tuple(spans)),
        out_shape=(jax.ShapeDtypeStruct((rows, first), BF16),) * 2,
        in_specs=[SMEM] + [hbm] * (3 * len(parts)),
        out_specs=(hbm, hbm),
        scratch_shapes=[pltpu.SemaphoreType.DMA((8 * len(parts),))],
        compiler_params=ROOM,
        cost_estimate=FREE,
        name="merge",
    )(plan, *[array for part in parts for array in part])


def join_kernel(places, *refs):
    count = len(places)
    sems = refs[-1]
    outs = refs[-3:-1]
    parts = refs[-3 - 2 * count : -3]
    copies = []
    for n in range(2):
        for i, (first, cols) in enumerate(places):
            copies.append(
                pltpu.make_async_copy(parts[n * count + i], outs[n].at[:, pl.ds(first, cols)], sems.at[n * count + i])
            )
    for copy in copies:
        copy.start()
    for copy in copies:
        copy.wait()


def make_join(width, first, nexts, returns, into=()):
    rows = nexts[0].shape[0]
    places = []
    for part in nexts:
        places.append((first, part.shape[1]))
        first += part.shape[1]
    hbm = pl.BlockSpec(memory_space=pl.ANY)
    return pl.pallas_call(
        functools.partial(join_kernel, tuple(places)),
        out_shape=(jax.ShapeDtypeStruct((rows, width), BF16),) * 2,
        in_specs=[hbm] * (len(into) + 2 * len(nexts)),
        out_specs=(hbm, hbm),
        scratch_shapes=[pltpu.SemaphoreType.DMA((2 * len(nexts),))],
        input_output_aliases={i: i for i in range(len(into))},
        compiler_params=ROOM,
        cost_estimate=FREE,
        name="join",
    )(*into, *nexts, *returns)


VMEM = pl.BlockSpec(memory_space=pltpu.VMEM)


def grad_down_kernel(x_ref, low_ref, low2_ref, high_ref, high2_ref, g_ref, *refs):
    got_refs, to_ref = refs[:-1], refs[-1]
    rows = x_ref.shape[0]
    dpre = [(low[rows:, :].astype(F32) * 0.5).astype(BF16) for low in (low_ref, low2_ref)]
    rinv = [high[...].T[:, 0:1] for high in (high_ref, high2_ref)]
    first = 0
    for got_ref in got_refs:
        at = slice(first, first + got_ref.shape[1])
        first = at.stop
        g = g_ref[:, at]
        own = (x_ref[:, at].astype(F32) * rinv[0] * g).astype(BF16)
        other = (got_ref[:rows, :].astype(F32) * rinv[1] * g).astype(BF16)
        to_ref[at, :] = dot(own, dpre[0], ((0,), (0,))) + dot(other, dpre[1], ((0,), (0,)))


def make_grad_down(x, got, low, low2, high, high2, g):
    return pl.pallas_call(
        grad_down_kernel,
        out_shape=jax.ShapeDtypeStruct((x.shape[1], low.shape[1]), F32),
        in_specs=[VMEM] * (6 + len(got)),
        out_specs=VMEM,
        compiler_params=ROOM,
        cost_estimate=FREE,
        name="grad_down",
    )(x, low, low2, high, high2, g, *got)


def turned_act(plan_ref, low2_ref, j, blk):
    at = pl.ds(pl.multiple_of(plan_ref[20 + j] * blk, blk), blk)
    return (low2_ref[at, :].astype(F32) * 0.5).T.astype(BF16)


def grad_up_kernel(plan_ref, dy_ref, low_ref, low2_ref, *refs):
    got_refs, to_ref = refs[:-1], refs[-1]
    rows = dy_ref.shape[0]
    blk = rows // 4
    own = (low_ref[:rows, :].astype(F32) * 0.5).T.astype(BF16)
    other = jnp.concatenate([turned_act(plan_ref, low2_ref, j, blk) for j in range(3)], axis=1)
    first = 0
    for got_ref in got_refs:
        at = slice(first, first + got_ref.shape[1])
        first = at.stop
        to_ref[:, at] = dot(own, dy_ref[:, at], ((1,), (0,))) + dot(
            other, got_ref[rows : rows + 3 * blk, :], ((1,), (0,))
        )


def make_grad_up(plan, dy, got, low, low2):
    return pl.pallas_call(
        grad_up_kernel,
        out_shape=jax.ShapeDtypeStruct((low.shape[1], dy.shape[1]), F32),
        in_specs=[SMEM] + [VMEM] * (3 + len(got)),
        out_specs=VMEM,
        compiler_params=ROOM,
        cost_estimate=FREE,
        name="grad_up",
    )(plan, dy, low, low2, *got)


def grad_up_late_kernel(plan_ref, so_far_ref, late_ref, low2_ref, to_ref):
    blk = late_ref.shape[0]
    act = turned_act(plan_ref, low2_ref, 3, blk)
    to_ref[...] = so_far_ref[...] + dot(act, late_ref[...], ((1,), (0,)))


def make_grad_up_late(plan, so_far, late, low2):
    rank, width = so_far.shape
    blk = late.shape[0]
    tile = 2 * TILE
    return pl.pallas_call(
        grad_up_late_kernel,
        grid=(width // tile,),
        out_shape=jax.ShapeDtypeStruct((rank, width), F32),
        in_specs=[SMEM, column(rank, 0, tile), column(blk, 0, tile), whole(low2.shape)],
        out_specs=column(rank, 0, tile),
        input_output_aliases={1: 0},
        compiler_params=ROOM,
        cost_estimate=FREE,
        name="grad_up_late",
    )(plan, so_far, late, low2)


def four_peers(inputs, out_grad, gains, down_proj, up_proj, wiring, pair_mask):
    x, dy, down, up = inputs[0, 0], out_grad[0, 0], down_proj[0], up_proj[0]
    width = x.shape[1]
    count = len(CHUNKS)
    starts = [sum(CHUNKS[:c]) for c in range(count + 1)]
    plan, choice, low, high, *outs, late = make_open(
        [n * TILE for n in CHUNKS], wiring, pair_mask, gains, x, dy, down, up
    )
    choice = choice[0]

    def stage(number, cap, mask, state):
        exchange, route = STAGES[number]
        if number == 0:
            held = {}
            late2 = swapped(late, "peer", mask) if cap == 4 else late
        else:
            low2, high2, late2, held = state
        held, parts, backs, sent = dict(held), [], {}, plan

        def send_on(c):
            ready = [source[d] for source, d in ((held, c - DEPTH), (backs, c - LAG)) if d in source]
            held[c] = swapped(after(outs[c], *ready) if ready else outs[c], "peer", mask)

        waiting = list(exchange)
        while waiting and (waiting[0] < exchange[0] + DEPTH):
            send_on(waiting.pop(0))
        if number == 0:
            low2, high2 = make_unpack(held[0], low, high)
        common = (low, low2, high, high2)
        for c in route:
            send, keep_f, keep_b = make_rows(
                cap, starts[c], CHUNKS[c], after(plan, sent), x, dy, held[c], *common, up, down, gains, late2
            )
            backs[c] = swapped(send, "peer", 1 if mask >= 2 else 2)
            parts.append((keep_f, keep_b, backs[c]))
            sent = send
            if waiting:
                send_on(waiting.pop(0))
        while waiting:
            send_on(waiting.pop(0))
        grads = ()
        if number == len(STAGES) - 1 and cap == 3:
            late2 = swapped(after(late, held[count - 1]), "peer", mask)
        if number == len(STAGES) - 1:
            blocks = [held[c] for c in range(count)]
            up_grad = make_grad_up(after(plan, sent), dy, blocks, low, low2)
            grads = up_grad, make_grad_down(after(x, up_grad), blocks, *common, gains)
        merged = make_merge(cap, after(plan, sent), parts)
        return merged, (low2, high2) if number == 0 else (), late2, {c: held[c] for c in exchange}, grads

    state = None
    nexts, returns = [], []
    for number in range(len(STAGES)):
        branches = [functools.partial(stage, number, cap, m) for cap in (3, 4) for m in (1, 2, 3)]
        (f, b), made, late2, arrived, grads = lax.switch(choice, branches, state)
        if number == 0:
            low2, high2 = made
            held = {}
        held = {**held, **arrived}
        state = (low2, high2, late2, held)
        if number:
            f, b = after(f, nexts[-1], returns[-1]), after(b, nexts[-1], returns[-1])
        nexts.append(passed_along(f, "section", 1))
        returns.append(passed_along(b, "section", -1))
    so_far, grad_down = grads
    grad_up = make_grad_up_late(plan, after(so_far, f, b), late2, low2)
    joined = make_join(width, 0, [after(nexts[0], f, b), *nexts[1:-1]], returns[:-1])
    done = sum(part.shape[1] for part in nexts[:-1])
    next_rows, return_rows = make_join(width, done, nexts[-1:], returns[-1:], into=joined)
    return next_rows[None, None], return_rows[None, None], grad_down[None, None], grad_up[None, None]


def adapter(x, dy, g, down, up):
    xf = x.astype(F32)
    rinv = lax.rsqrt(jnp.mean(xf * xf, axis=-1, keepdims=True) + 1e-05)
    normed = (xf * rinv * g).astype(BF16)
    pre = dot(normed, down, ((1,), (0,)))
    sig = jax.nn.sigmoid(pre)
    act = (pre * sig).astype(BF16)
    dact = dot(dy, up, ((1,), (1,)))
    dpre = (dact * sig * (1.0 + pre * (1.0 - sig))).astype(BF16)
    inner = jnp.sum(dpre.astype(F32) * pre, axis=-1, keepdims=True) / x.shape[1]
    return act, dpre, rinv, rinv * rinv * inner


def layer(x, dy, g, down, up):
    xf = x.astype(F32)
    act, dpre, rinv, weight = adapter(x, dy, g, down, up)
    normed = (xf * rinv * g).astype(BF16)
    out = (xf + dot(act, up, ((1,), (0,)))).astype(BF16)
    gup = dot(act, dy, ((0,), (0,))).astype(BF16)
    gdown = dot(normed, dpre, ((0,), (0,))).astype(BF16)
    dnorm = dot(dpre, down, ((1,), (1,))) * g
    dx = (dy.astype(F32) + rinv * dnorm - xf * weight).astype(BF16)
    return (out, dx, gdown, gup)


def pack_blocks(blocks, counts_vec, first_vec, slots):
    peers = counts_vec.shape[0]
    nblocks = blocks.shape[0]
    place = jnp.arange(slots, dtype=jnp.int32)
    source = first_vec[:, None] + place[None, :]
    valid = place[None, :] < counts_vec[:, None]
    select = (source[:, :, None] == jnp.arange(nblocks, dtype=jnp.int32)[None, None, :]) & valid[:, :, None]
    select = select.astype(BF16).reshape(peers * slots, nblocks)
    return jnp.dot(select, blocks, preferred_element_type=F32).astype(BF16)


def unpack_blocks(received, counts_vec, first_vec, slots, nblocks):
    place = jnp.arange(slots, dtype=jnp.int32)
    target = (first_vec[:, None] + place[None, :]).reshape(-1)
    valid = (place[None, :] < counts_vec[:, None]).reshape(-1)
    select = (target[None, :] == jnp.arange(nblocks, dtype=jnp.int32)[:, None]) & valid[None, :]
    return jnp.dot(select.astype(BF16), received, preferred_element_type=F32).astype(BF16)


def any_peers(inputs, out_grad, gains, down_proj, up_proj, wiring, pair_mask):
    sections = lax.axis_size("section")
    nblocks = lax.axis_size("peer")
    section = lax.axis_index("section")
    peer = lax.axis_index("peer")
    x = inputs[0, 0]
    rows, width = x.shape
    out, dx, gdown, gup = layer(x, out_grad[0, 0], gains[0], down_proj[0], up_proj[0])
    blk_rows = rows // nblocks
    here = lax.dynamic_index_in_dim(wiring, section, 0, keepdims=False)
    before = lax.dynamic_index_in_dim(wiring, (section + sections - 1) % sections, 0, keepdims=False)
    here_start = jnp.cumsum(here, axis=1) - here
    before_col = jnp.cumsum(before, axis=0) - before
    out_blocks = out.reshape(nblocks, blk_rows * width)
    dx_blocks = dx.reshape(nblocks, blk_rows * width)
    fwd_buf = pack_blocks(out_blocks, here[peer], here_start[peer], CAP)
    back_buf = pack_blocks(dx_blocks, before[:, peer], before_col[:, peer], CAP)
    moved = passed_along(fwd_buf, "section", 1)
    got_fwd = lax.all_to_all(moved, "peer", split_axis=0, concat_axis=0, tiled=True)
    next_rows = unpack_blocks(got_fwd, before[:, peer], before_col[:, peer], CAP, nblocks)
    moved_back = passed_along(back_buf, "section", -1)
    got_back = lax.all_to_all(moved_back, "peer", split_axis=0, concat_axis=0, tiled=True)
    return_rows = unpack_blocks(got_back, here[peer], here_start[peer], CAP, nblocks)
    mask_value = pair_mask[section]
    other_down, other_up = (gdown, gup)
    for bit in range(nblocks.bit_length() - 1):
        swapped_down, swapped_up = swapped((other_down, other_up), "peer", 1 << bit)
        take = jnp.bitwise_and(jnp.right_shift(mask_value, bit), 1) == 1
        other_down = jnp.where(take, swapped_down, other_down)
        other_up = jnp.where(take, swapped_up, other_up)
    grad_down = (gdown.astype(F32) + other_down.astype(F32)) * 0.5
    grad_up = (gup.astype(F32) + other_up.astype(F32)) * 0.5
    return (
        next_rows.reshape(1, 1, rows, width),
        return_rows.reshape(1, 1, rows, width),
        grad_down[None, None],
        grad_up[None, None],
    )


def solution(mesh):
    whole = P("section", "peer", None, None)
    return jax.shard_map(
        four_peers if mesh.shape["peer"] == 4 else any_peers,
        mesh=mesh,
        in_specs=(whole, whole, P("section", None), P("section", None, None), P("section", None, None), P(), P()),
        out_specs=(whole,) * 4,
        check_vma=False,
    )
```

```python
import functools

import jax
import jax.numpy as jnp
from jax import lax
from jax.experimental import pallas as pl
from jax.experimental.pallas import tpu as pltpu
from jax.sharding import PartitionSpec as P

CAP = 2
TILE = 512
CHUNKS = (2, 2, 2, 2, 2)
STAGES = (((0, 1, 2), (0, 1)), ((3, 4), (2, 3)), ((), (4,)))
DEPTH, LAG = 1, 2
F32, BF16 = jnp.float32, jnp.bfloat16


def passed_along(block, axis, distance):
    devices = range(lax.axis_size(axis))
    route = [((i - distance) % len(devices), i) for i in devices]
    return lax.ppermute(block, axis, route)


def swapped(block, axis, mask):
    count = lax.axis_size(axis)
    return lax.ppermute(block, axis, [(i, i ^ mask) for i in range(count) if i ^ mask < count])


def after(value, *others):
    return lax.optimization_barrier((value, *others))[0]


def dot(a, b, dims):
    return lax.dot_general(a, b, (dims, ((), ())), preferred_element_type=F32)


PIECE = 1024
FREE = pl.CostEstimate(flops=0, bytes_accessed=0, transcendentals=0)
ROOM = pltpu.CompilerParams(vmem_limit_bytes=32 * 2**20)
SMEM = pl.BlockSpec(memory_space=pltpu.SMEM)


def open_kernel(widths, wiring_ref, mask_ref, g_ref, x_ref, dy_ref, down_ref, up_ref, plan_ref, choice_ref, low_ref,
                high_ref, *refs):
    outs, late_ref = refs[: len(widths)], refs[len(widths)]
    x_scr, dy_scr, down_scr, up_scr, extra, in_sems, out_sems, extra_sems = refs[len(widths) + 1 :]
    rows, width = x_ref.shape
    rank = up_ref.shape[0]
    pieces = [slice(i, i + PIECE) for i in range(0, width, PIECE)]
    loads = []
    for i, at in enumerate(pieces):
        pairs = ((x_ref.at[:, at], x_scr.at[:, at]), (dy_ref.at[:, at], dy_scr.at[:, at]),
                 (down_ref.at[at, :], down_scr.at[at, :]), (up_ref.at[:, at], up_scr.at[:, at]))
        loads.append([pltpu.make_async_copy(s, t, in_sems.at[4 * i + n]) for n, (s, t) in enumerate(pairs)])
    for some in loads:
        for copy in some:
            copy.start()
    section, peer = lax.axis_index("section"), lax.axis_index("peer")
    count = wiring_ref.shape[0]
    before = lax.rem(section + count - 1, count)
    mask = mask_ref[section]
    match = peer ^ mask
    other = peer ^ jnp.where(mask >= 2, 1, 2)

    def sources(back, q):
        at = [jnp.int32(0)] * 4
        block = [jnp.int32(0)] * 4
        cum = jnp.int32(0)
        for i in range(4):
            first = jnp.int32(0)
            for j in range(4):
                if back:
                    first += jnp.where(j < q, wiring_ref[before, j, i], 0)
                else:
                    first += jnp.where(j < q, wiring_ref[section, i, j], 0)
            amount = wiring_ref[before, q, i] if back else wiring_ref[section, i, q]
            for k in range(4):
                inside = (cum <= k) & (k < cum + amount)
                at[k] = jnp.where(inside, i, at[k])
                block[k] = jnp.where(inside, first + k - cum, block[k])
            cum += amount
        held = [((a == peer) | (a == match)).astype(jnp.int32) for a in at]
        index = [jnp.where(a == peer, b, 4 + b) for a, b in zip(at, block)]
        return held, index

    for n, back in enumerate((False, True)):
        held, index = sources(back, other)
        order = jnp.int32(0)
        orders = []
        for k in range(4):
            orders.append(order)
            order += held[k]
        for j in range(4):
            pick = jnp.int32(0)
            for k in range(4):
                pick += jnp.where((held[k] == 1) & (orders[k] == j), index[k], 0)
            plan_ref[4 * n + j] = pick
        held, index = sources(back, peer)
        order = jnp.int32(0)
        for k in range(4):
            plan_ref[8 + 4 * n + k] = jnp.where(held[k] == 1, index[k], 8 + order)
            order += 1 - held[k]
    twos = jnp.int32(0)
    for at in (section, before):
        for i in range(4):
            for j in range(4):
                twos += jnp.where(wiring_ref[at, i, j] == 2, 1, 0)
    choice_ref[0] = mask - 1 + jnp.where(twos > 8, 3, 0)
    for n, (owner, to) in enumerate(((peer, match), (match, peer))):
        wanted, cum = [jnp.int32(0)] * 4, jnp.int32(0)
        for q in range(4):
            amount = wiring_ref[before, q, owner]
            near = ((q == to) | (q == (to ^ jnp.where(mask >= 2, 1, 2)))).astype(jnp.int32)
            for k in range(4):
                wanted[k] = jnp.where((cum <= k) & (k < cum + amount), near, wanted[k])
            cum += amount
        total = sum(wanted)
        ahead, behind = jnp.int32(0), jnp.int32(0)
        slots = []
        for k in range(4):
            slots.append(jnp.where(wanted[k] == 1, ahead, total + behind))
            ahead += wanted[k]
            behind += 1 - wanted[k]
        for j in range(4):
            plan_ref[16 + 4 * n + j] = sum(jnp.where(slots[k] == j, k, 0) for k in range(4))

    blk = rows // 4
    stores, first = [], 0
    for c, cols in enumerate(widths):
        at = pl.ds(first, cols)
        first += cols
        sem = out_sems.at[4 * c]
        stores.append((first, pltpu.make_async_copy(x_scr.at[:, at], outs[c].at[pl.ds(0, rows), :], sem)))
        for j in range(3):
            from_rows = pl.ds(pl.multiple_of(plan_ref[16 + j] * blk, blk), blk)
            to = outs[c].at[pl.ds(rows + j * blk, blk), :]
            stores.append((first, pltpu.make_async_copy(dy_scr.at[from_rows, at], to, out_sems.at[4 * c + 1 + j])))
    from_rows = pl.ds(pl.multiple_of(plan_ref[19] * blk, blk), blk)
    stores.append((width, pltpu.make_async_copy(dy_scr.at[from_rows, :], late_ref, extra_sems.at[1])))

    square = jnp.zeros((rows, 1), F32)
    pre = jnp.zeros((rows, rank), F32)
    dact = jnp.zeros((rows, rank), F32)
    for some, at in zip(loads, pieces):
        for copy in some:
            copy.wait()
        for end, copy in stores:
            if at.start < end <= at.stop:
                copy.start()
        x = x_scr[:, at].astype(F32)
        square += jnp.sum(x * x, axis=1, keepdims=True)
        dact += dot(dy_scr[:, at], up_scr[:, at], ((1,), (1,)))
    rinv = lax.rsqrt(square / width + 1e-05)
    for at in pieces:
        normed = (x_scr[:, at].astype(F32) * rinv * g_ref[:, at]).astype(BF16)
        pre += dot(normed, down_scr[at, :], ((1,), (0,)))
    v = pre
    sig = jax.nn.sigmoid(v)
    act = (v * sig).astype(BF16)
    dpre = (dact * sig * (1.0 + v * (1.0 - sig))).astype(BF16)
    inner = jnp.sum(dpre.astype(F32) * v, axis=1, keepdims=True) / width
    weight = rinv * rinv * inner
    low_ref[:rows, :] = act
    low_ref[rows:, :] = dpre
    lane = lax.broadcasted_iota(jnp.int32, (rows, rows), 1)
    high = jnp.where(lane == 0, rinv, weight).T[:8, :]
    high_ref[...] = high
    bands = widths[0] // rank
    band = 2 * rows // bands
    for j in range(bands):
        from_ref = act if (j + 1) * band <= rows else dpre
        start = j * band % rows
        extra[:band, j * rank : (j + 1) * rank] = from_ref[start : start + band, :]
    rest = high
    parts = []
    for _ in range(3):
        part = rest.astype(BF16)
        parts.append(part)
        rest = rest - part.astype(F32)
    extra[band:, :] = jnp.zeros_like(extra[band:, :])
    extra[band : band + 16, 0:rows] = jnp.concatenate([parts[0], parts[1]], axis=0)
    extra[band : band + 16, rows : 2 * rows] = jnp.concatenate([parts[2], parts[2]], axis=0)
    last = pltpu.make_async_copy(extra, outs[0].at[pl.ds(rows + 3 * blk, band + 16), :], extra_sems.at[0])
    last.start()
    for _, copy in stores:
        copy.wait()
    last.wait()


def make_open(widths, wiring, pair_mask, g, x, dy, down, up):
    rows, width = x.shape
    rank = up.shape[0]
    band = 2 * rows * rank // widths[0]
    hbm = pl.BlockSpec(memory_space=pl.ANY)
    vmem = pl.BlockSpec(memory_space=pltpu.VMEM)
    sent = rows + 3 * (rows // 4)
    tall = [sent + band + 16] + [sent] * (len(widths) - 1)
    return pl.pallas_call(
        functools.partial(open_kernel, widths),
        out_shape=[
            jax.ShapeDtypeStruct((24,), jnp.int32),
            jax.ShapeDtypeStruct((1,), jnp.int32),
            jax.ShapeDtypeStruct((2 * rows, rank), BF16),
            jax.ShapeDtypeStruct((8, rows), F32),
        ] + [jax.ShapeDtypeStruct((n, cols), BF16) for n, cols in zip(tall, widths)]
        + [jax.ShapeDtypeStruct((rows // 4, width), BF16)],
        in_specs=[SMEM, SMEM, vmem, hbm, hbm, hbm, hbm],
        out_specs=[SMEM, SMEM, vmem, vmem] + [hbm] * (len(widths) + 1),
        scratch_shapes=[
            pltpu.VMEM((rows, width), BF16), pltpu.VMEM((rows, width), BF16),
            pltpu.VMEM((width, rank), BF16), pltpu.VMEM((rank, width), BF16),
            pltpu.VMEM((band + 16, widths[0]), BF16),
            pltpu.SemaphoreType.DMA((4 * (width // PIECE),)), pltpu.SemaphoreType.DMA((4 * len(widths),)),
            pltpu.SemaphoreType.DMA((2,)),
        ],
        compiler_params=ROOM,
        cost_estimate=FREE,
        name="open",
    )(wiring, pair_mask, g, x, dy, down, up)


def unpack_kernel(got_ref, low_ref, high_ref):
    rows2, rank = low_ref.shape
    bands = got_ref.shape[1] // rank
    band = rows2 // bands
    rows = rows2 // 2
    first = got_ref.shape[0] - band - 16
    for j in range(bands):
        low_ref[j * band : (j + 1) * band, :] = got_ref[first : first + band, j * rank : (j + 1) * rank]
    parts = got_ref[first + band :, :].astype(F32)
    high_ref[...] = parts[0:8, 0:rows] + parts[8:16, 0:rows] + parts[0:8, rows : 2 * rows]


def make_unpack(got, low, high):
    vmem = pl.BlockSpec(memory_space=pltpu.VMEM)
    return pl.pallas_call(
        unpack_kernel,
        out_shape=(jax.ShapeDtypeStruct(low.shape, BF16), jax.ShapeDtypeStruct(high.shape, F32)),
        in_specs=[vmem],
        out_specs=(vmem, vmem),
        compiler_params=ROOM,
        cost_estimate=FREE,
        name="unpack",
    )(got)


def whole(shape):
    return pl.BlockSpec(shape, lambda i: (0,) * len(shape))


def column(rows, first=0, tile=TILE):
    return pl.BlockSpec((rows, tile), lambda i: (0, first + i))


def chunk(rows, start, end, tile=TILE):
    return pl.BlockSpec((rows, tile), lambda i: (0, jnp.clip(i - start, 0, end - start - 1)))


def rows_kernel(cap, blk, plan_ref, x_ref, dy_ref, got_ref, low_ref, low2_ref, high_ref, high2_ref, up_ref, down_ref,
                g_ref, *refs):
    late_refs = refs[: cap - 3]
    send_ref, keep_f_ref, keep_b_ref, out_scr, dx_scr, rest_scr = refs[cap - 3 :]
    rows = x_ref.shape[0]
    for half in range(2):
        part = pl.ds(half * rows, rows)
        x = (x_ref[...] if half == 0 else got_ref[:rows, :]).astype(F32)
        low = low_ref if half == 0 else low2_ref
        stat = (high_ref if half == 0 else high2_ref)[...].T
        out = x + dot(low[:rows, :], up_ref[...], ((1,), (0,)))
        out_scr[part, :] = out.astype(BF16)
        dn = dot(low[rows:, :], down_ref[...], ((1,), (1,))) * g_ref[...]
        rest = stat[:, 0:1] * dn - x * stat[:, 1:2]
        if half == 0:
            dx_scr[part, :] = (dy_ref[...].astype(F32) + rest).astype(BF16)
        else:
            rest_scr[...] = rest
    for j in range(cap):
        dy = late_refs[0][...] if j == 3 else got_ref[rows + j * blk : rows + (j + 1) * blk, :]
        at = pl.multiple_of(plan_ref[20 + j] * blk, blk)
        dx_scr[pl.ds(rows + at, blk), :] = (dy.astype(F32) + rest_scr[pl.ds(at, blk), :]).astype(BF16)

    def block_of(scr, index):
        return scr[pl.ds(pl.multiple_of(index * blk, blk), blk), :]

    for n, scr in enumerate((out_scr, dx_scr)):
        for j in range(cap):
            send_ref[pl.ds((n * cap + j) * blk, blk), :] = block_of(scr, plan_ref[4 * n + j])
    for n, (scr, keep_ref) in enumerate(((out_scr, keep_f_ref), (dx_scr, keep_b_ref))):
        for k in range(4):
            keep_ref[pl.ds(k * blk, blk), :] = block_of(scr, jnp.minimum(plan_ref[8 + 4 * n + k], 7))


def make_rows(cap, first, tiles, plan, x, dy, got, low, low2, high, high2, up, down, g, late):
    rows, width = x.shape
    rank = up.shape[0]
    blk = rows // 4
    cols = tiles * TILE
    return pl.pallas_call(
        functools.partial(rows_kernel, cap, blk),
        grid=(tiles,),
        out_shape=(
            jax.ShapeDtypeStruct((2 * cap * blk, cols), BF16),
            jax.ShapeDtypeStruct((rows, cols), BF16),
            jax.ShapeDtypeStruct((rows, cols), BF16),
        ),
        in_specs=[
            SMEM, column(rows, first), column(rows, first), column(rows + 3 * blk),
            whole(low.shape), whole(low.shape), whole(high.shape), whole(high.shape),
            column(rank, first), pl.BlockSpec((TILE, rank), lambda i: (first + i, 0)), column(1, first),
        ] + [column(blk, first)] * (cap - 3),
        out_specs=(column(2 * cap * blk), column(rows), column(rows)),
        scratch_shapes=[
            pltpu.VMEM((2 * rows, TILE), BF16), pltpu.VMEM((2 * rows, TILE), BF16), pltpu.VMEM((rows, TILE), F32)
        ],
        compiler_params=ROOM,
        cost_estimate=FREE,
        name="rows",
    )(plan, x, dy, got, low, low2, high, high2, up, down, g, *[late] * (cap - 3))


def merge_kernel(cap, blk, spans, plan_ref, *refs):
    outs, sems = refs[-3:-1], refs[-1]
    waits = []
    for c, (first, cols) in enumerate(spans):
        keeps, got = refs[3 * c : 3 * c + 2], refs[3 * c + 2]
        for n in range(2):
            for k in range(4):
                index = plan_ref[8 + 4 * n + k]
                rows = pl.ds(k * blk, blk)
                to = outs[n].at[rows, pl.ds(first, cols)]
                sem = sems.at[8 * c + 4 * n + k]
                row = pl.multiple_of((n * cap + jnp.clip(index - 8, 0, cap - 1)) * blk, blk)
                here = pltpu.make_async_copy(keeps[n].at[rows, :], to, sem)
                there = pltpu.make_async_copy(got.at[pl.ds(row, blk), :], to, sem)

                @pl.when(index < 8)
                def _():
                    here.start()

                @pl.when(index >= 8)
                def _():
                    there.start()

                waits.append(here)
    for copy in waits:
        copy.wait()


def make_merge(cap, plan, parts):
    rows = parts[0][0].shape[0]
    spans, first = [], 0
    for keep_f, _, _ in parts:
        spans.append((first, keep_f.shape[1]))
        first += keep_f.shape[1]
    hbm = pl.BlockSpec(memory_space=pl.ANY)
    return pl.pallas_call(
        functools.partial(merge_kernel, cap, rows // 4, tuple(spans)),
        out_shape=(jax.ShapeDtypeStruct((rows, first), BF16),) * 2,
        in_specs=[SMEM] + [hbm] * (3 * len(parts)),
        out_specs=(hbm, hbm),
        scratch_shapes=[pltpu.SemaphoreType.DMA((8 * len(parts),))],
        compiler_params=ROOM,
        cost_estimate=FREE,
        name="merge",
    )(plan, *[array for part in parts for array in part])


def join_kernel(places, *refs):
    count = len(places)
    sems = refs[-1]
    outs = refs[-3:-1]
    parts = refs[-3 - 2 * count : -3]
    copies = []
    for n in range(2):
        for i, (first, cols) in enumerate(places):
            copies.append(
                pltpu.make_async_copy(parts[n * count + i], outs[n].at[:, pl.ds(first, cols)], sems.at[n * count + i])
            )
    for copy in copies:
        copy.start()
    for copy in copies:
        copy.wait()


def make_join(width, first, nexts, returns, into=()):
    rows = nexts[0].shape[0]
    places = []
    for part in nexts:
        places.append((first, part.shape[1]))
        first += part.shape[1]
    hbm = pl.BlockSpec(memory_space=pl.ANY)
    return pl.pallas_call(
        functools.partial(join_kernel, tuple(places)),
        out_shape=(jax.ShapeDtypeStruct((rows, width), BF16),) * 2,
        in_specs=[hbm] * (len(into) + 2 * len(nexts)),
        out_specs=(hbm, hbm),
        scratch_shapes=[pltpu.SemaphoreType.DMA((2 * len(nexts),))],
        input_output_aliases={i: i for i in range(len(into))},
        compiler_params=ROOM,
        cost_estimate=FREE,
        name="join",
    )(*into, *nexts, *returns)


VMEM = pl.BlockSpec(memory_space=pltpu.VMEM)


def grad_down_kernel(x_ref, low_ref, low2_ref, high_ref, high2_ref, g_ref, *refs):
    got_refs, to_ref = refs[:-1], refs[-1]
    rows = x_ref.shape[0]
    dpre = [(low[rows:, :].astype(F32) * 0.5).astype(BF16) for low in (low_ref, low2_ref)]
    rinv = [high[...].T[:, 0:1] for high in (high_ref, high2_ref)]
    first = 0
    for got_ref in got_refs:
        at = slice(first, first + got_ref.shape[1])
        first = at.stop
        g = g_ref[:, at]
        own = (x_ref[:, at].astype(F32) * rinv[0] * g).astype(BF16)
        other = (got_ref[:rows, :].astype(F32) * rinv[1] * g).astype(BF16)
        to_ref[at, :] = dot(own, dpre[0], ((0,), (0,))) + dot(other, dpre[1], ((0,), (0,)))


def make_grad_down(x, got, low, low2, high, high2, g):
    return pl.pallas_call(
        grad_down_kernel,
        out_shape=jax.ShapeDtypeStruct((x.shape[1], low.shape[1]), F32),
        in_specs=[VMEM] * (6 + len(got)),
        out_specs=VMEM,
        compiler_params=ROOM,
        cost_estimate=FREE,
        name="grad_down",
    )(x, low, low2, high, high2, g, *got)


def last_kernel(places, starts, plan_ref, low_ref, low2_ref, dy_ref, late_ref, *refs):
    chunks, count = len(starts) - 1, len(places)
    got_refs = refs[:chunks]
    parts = refs[chunks : chunks + 2 * count]
    to_ref, next_ref, return_ref = refs[chunks + 2 * count : chunks + 2 * count + 3]
    dy_scr, other_scr, to_scr, part_sems, in_sems, out_sems = refs[chunks + 2 * count + 3 :]
    rows = dy_ref.shape[0]
    blk = rows // 4
    loads, stores = [], []
    for c, got_ref in enumerate(got_refs):
        at = slice(starts[c], starts[c + 1])
        pairs = (
            (dy_ref.at[:, at], dy_scr.at[:, at]),
            (got_ref.at[pl.ds(rows, 3 * blk), :], other_scr.at[pl.ds(0, 3 * blk), at]),
            (late_ref.at[:, at], other_scr.at[pl.ds(3 * blk, blk), at]),
        )
        loads.append([pltpu.make_async_copy(x, y, in_sems.at[3 * c + n]) for n, (x, y) in enumerate(pairs)])
        stores.append(pltpu.make_async_copy(to_scr.at[:, at], to_ref.at[:, at], out_sems.at[c]))
    for some in loads:
        for copy in some:
            copy.start()
    joins = []
    for n, out_ref in enumerate((next_ref, return_ref)):
        for i, (first, cols) in enumerate(places):
            sem = part_sems.at[n * count + i]
            joins.append(pltpu.make_async_copy(parts[n * count + i], out_ref.at[:, pl.ds(first, cols)], sem))
    for copy in joins:
        copy.start()
    own = (low_ref[:rows, :].astype(F32) * 0.5).T.astype(BF16)
    ats = [pl.ds(pl.multiple_of(plan_ref[20 + j] * blk, blk), blk) for j in range(4)]
    other = jnp.concatenate([(low2_ref[at, :].astype(F32) * 0.5).T.astype(BF16) for at in ats], axis=1)
    for c, some in enumerate(loads):
        for copy in some:
            copy.wait()
        at = slice(starts[c], starts[c + 1])
        to_scr[:, at] = dot(own, dy_scr[:, at], ((1,), (0,))) + dot(other, other_scr[:, at], ((1,), (0,)))
        stores[c].start()
    for copy in joins + stores:
        copy.wait()


def make_last(plan, dy, late, got, low, low2, nexts, returns):
    rows, width = dy.shape
    rank = low.shape[1]
    starts, places = [0], []
    for block in got:
        starts.append(starts[-1] + block.shape[1])
    first = 0
    for part in nexts:
        places.append((first, part.shape[1]))
        first += part.shape[1]
    hbm = pl.BlockSpec(memory_space=pl.ANY)
    routed = jax.ShapeDtypeStruct((rows, width), BF16)
    return pl.pallas_call(
        functools.partial(last_kernel, tuple(places), tuple(starts)),
        out_shape=(jax.ShapeDtypeStruct((rank, width), F32), routed, routed),
        in_specs=[SMEM, VMEM, VMEM] + [hbm] * (2 + len(got) + 2 * len(nexts)),
        out_specs=(hbm,) * 3,
        scratch_shapes=[
            pltpu.VMEM((rows, width), BF16), pltpu.VMEM((rows, width), BF16), pltpu.VMEM((rank, width), F32),
            pltpu.SemaphoreType.DMA((2 * len(nexts),)), pltpu.SemaphoreType.DMA((3 * len(got),)),
            pltpu.SemaphoreType.DMA((len(got),)),
        ],
        compiler_params=ROOM,
        cost_estimate=FREE,
        name="last",
    )(plan, low, low2, dy, late, *got, *nexts, *returns)


def four_peers(inputs, out_grad, gains, down_proj, up_proj, wiring, pair_mask):
    x, dy, down, up = inputs[0, 0], out_grad[0, 0], down_proj[0], up_proj[0]
    width = x.shape[1]
    count = len(CHUNKS)
    starts = [sum(CHUNKS[:c]) for c in range(count + 1)]
    plan, choice, low, high, *outs, late = make_open(
        [n * TILE for n in CHUNKS], wiring, pair_mask, gains, x, dy, down, up
    )
    choice = choice[0]

    def stage(number, cap, mask, state):
        exchange, route = STAGES[number]
        if number == 0:
            held = {}
            late2 = swapped(late, "peer", mask) if cap == 4 else late
        else:
            low2, high2, late2, held = state
        held, parts, backs, sent = dict(held), [], {}, plan

        def send_on(c):
            ready = [source[d] for source, d in ((held, c - DEPTH), (backs, c - LAG)) if d in source]
            held[c] = swapped(after(outs[c], *ready) if ready else outs[c], "peer", mask)

        waiting = list(exchange)
        while waiting and (waiting[0] < exchange[0] + DEPTH):
            send_on(waiting.pop(0))
        if number == 0:
            low2, high2 = make_unpack(held[0], low, high)
        common = (low, low2, high, high2)
        for c in route:
            send, keep_f, keep_b = make_rows(
                cap, starts[c], CHUNKS[c], after(plan, sent), x, dy, held[c], *common, up, down, gains, late2
            )
            backs[c] = swapped(send, "peer", 1 if mask >= 2 else 2)
            parts.append((keep_f, keep_b, backs[c]))
            sent = send
            if waiting:
                send_on(waiting.pop(0))
        while waiting:
            send_on(waiting.pop(0))
        grads = ()
        if number == len(STAGES) - 1 and cap == 3:
            late2 = swapped(after(late, held[count - 1]), "peer", mask)
        if number == len(STAGES) - 1:
            blocks = [held[c] for c in range(count)]
            grads = make_grad_down(after(x, sent), blocks, *common, gains)
        merged = make_merge(cap, after(plan, sent), parts)
        return merged, (low2, high2) if number == 0 else (), late2, {c: held[c] for c in exchange}, grads

    state = None
    nexts, returns = [], []
    for number in range(len(STAGES)):
        branches = [functools.partial(stage, number, cap, m) for cap in (3, 4) for m in (1, 2, 3)]
        (f, b), made, late2, arrived, grad_down = lax.switch(choice, branches, state)
        if number == 0:
            low2, high2 = made
            held = {}
        held = {**held, **arrived}
        state = (low2, high2, late2, held)
        if number:
            f, b = after(f, nexts[-1], returns[-1]), after(b, nexts[-1], returns[-1])
        nexts.append(passed_along(f, "section", 1))
        returns.append(passed_along(b, "section", -1))
    grad_up, *joined = make_last(
        plan, after(dy, f, b), late2, [held[c] for c in range(count)], low, low2, nexts[:-1], returns[:-1]
    )
    done = sum(part.shape[1] for part in nexts[:-1])
    next_rows, return_rows = make_join(width, done, nexts[-1:], returns[-1:], into=joined)
    return next_rows[None, None], return_rows[None, None], grad_down[None, None], grad_up[None, None]


def adapter(x, dy, g, down, up):
    xf = x.astype(F32)
    rinv = lax.rsqrt(jnp.mean(xf * xf, axis=-1, keepdims=True) + 1e-05)
    normed = (xf * rinv * g).astype(BF16)
    pre = dot(normed, down, ((1,), (0,)))
    sig = jax.nn.sigmoid(pre)
    act = (pre * sig).astype(BF16)
    dact = dot(dy, up, ((1,), (1,)))
    dpre = (dact * sig * (1.0 + pre * (1.0 - sig))).astype(BF16)
    inner = jnp.sum(dpre.astype(F32) * pre, axis=-1, keepdims=True) / x.shape[1]
    return act, dpre, rinv, rinv * rinv * inner


def layer(x, dy, g, down, up):
    xf = x.astype(F32)
    act, dpre, rinv, weight = adapter(x, dy, g, down, up)
    normed = (xf * rinv * g).astype(BF16)
    out = (xf + dot(act, up, ((1,), (0,)))).astype(BF16)
    gup = dot(act, dy, ((0,), (0,))).astype(BF16)
    gdown = dot(normed, dpre, ((0,), (0,))).astype(BF16)
    dnorm = dot(dpre, down, ((1,), (1,))) * g
    dx = (dy.astype(F32) + rinv * dnorm - xf * weight).astype(BF16)
    return (out, dx, gdown, gup)


def pack_blocks(blocks, counts_vec, first_vec, slots):
    peers = counts_vec.shape[0]
    nblocks = blocks.shape[0]
    place = jnp.arange(slots, dtype=jnp.int32)
    source = first_vec[:, None] + place[None, :]
    valid = place[None, :] < counts_vec[:, None]
    select = (source[:, :, None] == jnp.arange(nblocks, dtype=jnp.int32)[None, None, :]) & valid[:, :, None]
    select = select.astype(BF16).reshape(peers * slots, nblocks)
    return jnp.dot(select, blocks, preferred_element_type=F32).astype(BF16)


def unpack_blocks(received, counts_vec, first_vec, slots, nblocks):
    place = jnp.arange(slots, dtype=jnp.int32)
    target = (first_vec[:, None] + place[None, :]).reshape(-1)
    valid = (place[None, :] < counts_vec[:, None]).reshape(-1)
    select = (target[None, :] == jnp.arange(nblocks, dtype=jnp.int32)[:, None]) & valid[None, :]
    return jnp.dot(select.astype(BF16), received, preferred_element_type=F32).astype(BF16)


def any_peers(inputs, out_grad, gains, down_proj, up_proj, wiring, pair_mask):
    sections = lax.axis_size("section")
    nblocks = lax.axis_size("peer")
    section = lax.axis_index("section")
    peer = lax.axis_index("peer")
    x = inputs[0, 0]
    rows, width = x.shape
    out, dx, gdown, gup = layer(x, out_grad[0, 0], gains[0], down_proj[0], up_proj[0])
    blk_rows = rows // nblocks
    here = lax.dynamic_index_in_dim(wiring, section, 0, keepdims=False)
    before = lax.dynamic_index_in_dim(wiring, (section + sections - 1) % sections, 0, keepdims=False)
    here_start = jnp.cumsum(here, axis=1) - here
    before_col = jnp.cumsum(before, axis=0) - before
    out_blocks = out.reshape(nblocks, blk_rows * width)
    dx_blocks = dx.reshape(nblocks, blk_rows * width)
    fwd_buf = pack_blocks(out_blocks, here[peer], here_start[peer], CAP)
    back_buf = pack_blocks(dx_blocks, before[:, peer], before_col[:, peer], CAP)
    moved = passed_along(fwd_buf, "section", 1)
    got_fwd = lax.all_to_all(moved, "peer", split_axis=0, concat_axis=0, tiled=True)
    next_rows = unpack_blocks(got_fwd, before[:, peer], before_col[:, peer], CAP, nblocks)
    moved_back = passed_along(back_buf, "section", -1)
    got_back = lax.all_to_all(moved_back, "peer", split_axis=0, concat_axis=0, tiled=True)
    return_rows = unpack_blocks(got_back, here[peer], here_start[peer], CAP, nblocks)
    mask_value = pair_mask[section]
    other_down, other_up = (gdown, gup)
    for bit in range(nblocks.bit_length() - 1):
        swapped_down, swapped_up = swapped((other_down, other_up), "peer", 1 << bit)
        take = jnp.bitwise_and(jnp.right_shift(mask_value, bit), 1) == 1
        other_down = jnp.where(take, swapped_down, other_down)
        other_up = jnp.where(take, swapped_up, other_up)
    grad_down = (gdown.astype(F32) + other_down.astype(F32)) * 0.5
    grad_up = (gup.astype(F32) + other_up.astype(F32)) * 0.5
    return (
        next_rows.reshape(1, 1, rows, width),
        return_rows.reshape(1, 1, rows, width),
        grad_down[None, None],
        grad_up[None, None],
    )


def solution(mesh):
    whole = P("section", "peer", None, None)
    return jax.shard_map(
        four_peers if mesh.shape["peer"] == 4 else any_peers,
        mesh=mesh,
        in_specs=(whole, whole, P("section", None), P("section", None, None), P("section", None, None), P(), P()),
        out_specs=(whole,) * 4,
        check_vma=False,
    )
```

```python
import functools

import jax
import jax.numpy as jnp
from jax import lax
from jax.experimental import pallas as pl
from jax.experimental.pallas import tpu as pltpu
from jax.sharding import PartitionSpec as P

CAP = 2
TILE = 512
CHUNKS = (1, 2, 3, 2, 2)
STAGES = (((0, 1, 2), (0, 1)), ((3, 4), (2, 3)), ((), (4,)))
DEPTH, LAG = 1, 2
F32, BF16 = jnp.float32, jnp.bfloat16


def passed_along(block, axis, distance):
    devices = range(lax.axis_size(axis))
    route = [((i - distance) % len(devices), i) for i in devices]
    return lax.ppermute(block, axis, route)


def swapped(block, axis, mask):
    count = lax.axis_size(axis)
    return lax.ppermute(block, axis, [(i, i ^ mask) for i in range(count) if i ^ mask < count])


def after(value, *others):
    return lax.optimization_barrier((value, *others))[0]


def dot(a, b, dims):
    return lax.dot_general(a, b, (dims, ((), ())), preferred_element_type=F32)


PIECE = 1024
FREE = pl.CostEstimate(flops=0, bytes_accessed=0, transcendentals=0)
ROOM = pltpu.CompilerParams(vmem_limit_bytes=32 * 2**20)
SMEM = pl.BlockSpec(memory_space=pltpu.SMEM)


def open_kernel(widths, wiring_ref, mask_ref, g_ref, x_ref, dy_ref, down_ref, up_ref, plan_ref, choice_ref, low_ref,
                high_ref, *refs):
    outs, late_ref = refs[: len(widths)], refs[len(widths)]
    x_scr, dy_scr, down_scr, up_scr, extra, in_sems, out_sems, extra_sems = refs[len(widths) + 1 :]
    rows, width = x_ref.shape
    rank = up_ref.shape[0]
    pieces = [slice(i, i + PIECE) for i in range(0, width, PIECE)]
    loads = []
    for i, at in enumerate(pieces):
        pairs = ((x_ref.at[:, at], x_scr.at[:, at]), (dy_ref.at[:, at], dy_scr.at[:, at]),
                 (down_ref.at[at, :], down_scr.at[at, :]), (up_ref.at[:, at], up_scr.at[:, at]))
        loads.append([pltpu.make_async_copy(s, t, in_sems.at[4 * i + n]) for n, (s, t) in enumerate(pairs)])
    for some in loads:
        for copy in some:
            copy.start()
    section, peer = lax.axis_index("section"), lax.axis_index("peer")
    count = wiring_ref.shape[0]
    before = lax.rem(section + count - 1, count)
    mask = mask_ref[section]
    match = peer ^ mask
    other = peer ^ jnp.where(mask >= 2, 1, 2)

    def sources(back, q):
        at = [jnp.int32(0)] * 4
        block = [jnp.int32(0)] * 4
        cum = jnp.int32(0)
        for i in range(4):
            first = jnp.int32(0)
            for j in range(4):
                if back:
                    first += jnp.where(j < q, wiring_ref[before, j, i], 0)
                else:
                    first += jnp.where(j < q, wiring_ref[section, i, j], 0)
            amount = wiring_ref[before, q, i] if back else wiring_ref[section, i, q]
            for k in range(4):
                inside = (cum <= k) & (k < cum + amount)
                at[k] = jnp.where(inside, i, at[k])
                block[k] = jnp.where(inside, first + k - cum, block[k])
            cum += amount
        held = [((a == peer) | (a == match)).astype(jnp.int32) for a in at]
        index = [jnp.where(a == peer, b, 4 + b) for a, b in zip(at, block)]
        return held, index

    for n, back in enumerate((False, True)):
        held, index = sources(back, other)
        order = jnp.int32(0)
        orders = []
        for k in range(4):
            orders.append(order)
            order += held[k]
        for j in range(4):
            pick = jnp.int32(0)
            for k in range(4):
                pick += jnp.where((held[k] == 1) & (orders[k] == j), index[k], 0)
            plan_ref[4 * n + j] = pick
        held, index = sources(back, peer)
        order = jnp.int32(0)
        for k in range(4):
            plan_ref[8 + 4 * n + k] = jnp.where(held[k] == 1, index[k], 8 + order)
            order += 1 - held[k]
    twos = jnp.int32(0)
    for at in (section, before):
        for i in range(4):
            for j in range(4):
                twos += jnp.where(wiring_ref[at, i, j] == 2, 1, 0)
    choice_ref[0] = mask - 1 + jnp.where(twos > 8, 3, 0)
    for n, (owner, to) in enumerate(((peer, match), (match, peer))):
        wanted, cum = [jnp.int32(0)] * 4, jnp.int32(0)
        for q in range(4):
            amount = wiring_ref[before, q, owner]
            near = ((q == to) | (q == (to ^ jnp.where(mask >= 2, 1, 2)))).astype(jnp.int32)
            for k in range(4):
                wanted[k] = jnp.where((cum <= k) & (k < cum + amount), near, wanted[k])
            cum += amount
        total = sum(wanted)
        ahead, behind = jnp.int32(0), jnp.int32(0)
        slots = []
        for k in range(4):
            slots.append(jnp.where(wanted[k] == 1, ahead, total + behind))
            ahead += wanted[k]
            behind += 1 - wanted[k]
        for j in range(4):
            plan_ref[16 + 4 * n + j] = sum(jnp.where(slots[k] == j, k, 0) for k in range(4))

    blk = rows // 4
    stores, first = [], 0
    for c, cols in enumerate(widths):
        at = pl.ds(first, cols)
        first += cols
        sem = out_sems.at[4 * c]
        stores.append((first, pltpu.make_async_copy(x_scr.at[:, at], outs[c].at[pl.ds(0, rows), :], sem)))
        for j in range(3):
            from_rows = pl.ds(pl.multiple_of(plan_ref[16 + j] * blk, blk), blk)
            to = outs[c].at[pl.ds(rows + j * blk, blk), :]
            stores.append((first, pltpu.make_async_copy(dy_scr.at[from_rows, at], to, out_sems.at[4 * c + 1 + j])))
    from_rows = pl.ds(pl.multiple_of(plan_ref[19] * blk, blk), blk)
    stores.append((width, pltpu.make_async_copy(dy_scr.at[from_rows, :], late_ref, extra_sems.at[1])))

    square = jnp.zeros((rows, 1), F32)
    pre = jnp.zeros((rows, rank), F32)
    dact = jnp.zeros((rows, rank), F32)
    for some, at in zip(loads, pieces):
        for copy in some:
            copy.wait()
        for end, copy in stores:
            if at.start < end <= at.stop:
                copy.start()
        x = x_scr[:, at].astype(F32)
        square += jnp.sum(x * x, axis=1, keepdims=True)
        dact += dot(dy_scr[:, at], up_scr[:, at], ((1,), (1,)))
    rinv = lax.rsqrt(square / width + 1e-05)
    for at in pieces:
        normed = (x_scr[:, at].astype(F32) * rinv * g_ref[:, at]).astype(BF16)
        pre += dot(normed, down_scr[at, :], ((1,), (0,)))
    v = pre
    sig = jax.nn.sigmoid(v)
    act = (v * sig).astype(BF16)
    dpre = (dact * sig * (1.0 + v * (1.0 - sig))).astype(BF16)
    inner = jnp.sum(dpre.astype(F32) * v, axis=1, keepdims=True) / width
    weight = rinv * rinv * inner
    low_ref[:rows, :] = act
    low_ref[rows:, :] = dpre
    lane = lax.broadcasted_iota(jnp.int32, (rows, rows), 1)
    high = jnp.where(lane == 0, rinv, weight).T[:8, :]
    high_ref[...] = high
    bands = widths[0] // rank
    band = 2 * rows // bands
    for j in range(bands):
        from_ref = act if (j + 1) * band <= rows else dpre
        start = j * band % rows
        extra[:band, j * rank : (j + 1) * rank] = from_ref[start : start + band, :]
    rest = high
    parts = []
    for _ in range(3):
        part = rest.astype(BF16)
        parts.append(part)
        rest = rest - part.astype(F32)
    extra[band:, :] = jnp.zeros_like(extra[band:, :])
    extra[band : band + 16, 0:rows] = jnp.concatenate([parts[0], parts[1]], axis=0)
    extra[band : band + 16, rows : 2 * rows] = jnp.concatenate([parts[2], parts[2]], axis=0)
    last = pltpu.make_async_copy(extra, outs[0].at[pl.ds(rows + 3 * blk, band + 16), :], extra_sems.at[0])
    last.start()
    for _, copy in stores:
        copy.wait()
    last.wait()


def make_open(widths, wiring, pair_mask, g, x, dy, down, up):
    rows, width = x.shape
    rank = up.shape[0]
    band = 2 * rows * rank // widths[0]
    hbm = pl.BlockSpec(memory_space=pl.ANY)
    vmem = pl.BlockSpec(memory_space=pltpu.VMEM)
    sent = rows + 3 * (rows // 4)
    tall = [sent + band + 16] + [sent] * (len(widths) - 1)
    return pl.pallas_call(
        functools.partial(open_kernel, widths),
        out_shape=[
            jax.ShapeDtypeStruct((24,), jnp.int32),
            jax.ShapeDtypeStruct((1,), jnp.int32),
            jax.ShapeDtypeStruct((2 * rows, rank), BF16),
            jax.ShapeDtypeStruct((8, rows), F32),
        ] + [jax.ShapeDtypeStruct((n, cols), BF16) for n, cols in zip(tall, widths)]
        + [jax.ShapeDtypeStruct((rows // 4, width), BF16)],
        in_specs=[SMEM, SMEM, vmem, hbm, hbm, hbm, hbm],
        out_specs=[SMEM, SMEM, vmem, vmem] + [hbm] * (len(widths) + 1),
        scratch_shapes=[
            pltpu.VMEM((rows, width), BF16), pltpu.VMEM((rows, width), BF16),
            pltpu.VMEM((width, rank), BF16), pltpu.VMEM((rank, width), BF16),
            pltpu.VMEM((band + 16, widths[0]), BF16),
            pltpu.SemaphoreType.DMA((4 * (width // PIECE),)), pltpu.SemaphoreType.DMA((4 * len(widths),)),
            pltpu.SemaphoreType.DMA((2,)),
        ],
        compiler_params=ROOM,
        cost_estimate=FREE,
        name="open",
    )(wiring, pair_mask, g, x, dy, down, up)


def unpack_kernel(got_ref, low_ref, high_ref):
    rows2, rank = low_ref.shape
    bands = got_ref.shape[1] // rank
    band = rows2 // bands
    rows = rows2 // 2
    first = got_ref.shape[0] - band - 16
    for j in range(bands):
        low_ref[j * band : (j + 1) * band, :] = got_ref[first : first + band, j * rank : (j + 1) * rank]
    parts = got_ref[first + band :, :].astype(F32)
    high_ref[...] = parts[0:8, 0:rows] + parts[8:16, 0:rows] + parts[0:8, rows : 2 * rows]


def make_unpack(got, low, high):
    vmem = pl.BlockSpec(memory_space=pltpu.VMEM)
    return pl.pallas_call(
        unpack_kernel,
        out_shape=(jax.ShapeDtypeStruct(low.shape, BF16), jax.ShapeDtypeStruct(high.shape, F32)),
        in_specs=[vmem],
        out_specs=(vmem, vmem),
        compiler_params=ROOM,
        cost_estimate=FREE,
        name="unpack",
    )(got)


def whole(shape):
    return pl.BlockSpec(shape, lambda i: (0,) * len(shape))


def column(rows, first=0, tile=TILE):
    return pl.BlockSpec((rows, tile), lambda i: (0, first + i))


def chunk(rows, start, end, tile=TILE):
    return pl.BlockSpec((rows, tile), lambda i: (0, jnp.clip(i - start, 0, end - start - 1)))


def rows_kernel(cap, blk, plan_ref, x_ref, dy_ref, got_ref, low_ref, low2_ref, high_ref, high2_ref, up_ref, down_ref,
                g_ref, *refs):
    late_refs = refs[: cap - 3]
    send_ref, keep_f_ref, keep_b_ref, out_scr, dx_scr, rest_scr = refs[cap - 3 :]
    rows = x_ref.shape[0]
    for half in range(2):
        part = pl.ds(half * rows, rows)
        x = (x_ref[...] if half == 0 else got_ref[:rows, :]).astype(F32)
        low = low_ref if half == 0 else low2_ref
        stat = (high_ref if half == 0 else high2_ref)[...].T
        out = x + dot(low[:rows, :], up_ref[...], ((1,), (0,)))
        out_scr[part, :] = out.astype(BF16)
        dn = dot(low[rows:, :], down_ref[...], ((1,), (1,))) * g_ref[...]
        rest = stat[:, 0:1] * dn - x * stat[:, 1:2]
        if half == 0:
            dx_scr[part, :] = (dy_ref[...].astype(F32) + rest).astype(BF16)
        else:
            rest_scr[...] = rest
    for j in range(cap):
        dy = late_refs[0][...] if j == 3 else got_ref[rows + j * blk : rows + (j + 1) * blk, :]
        at = pl.multiple_of(plan_ref[20 + j] * blk, blk)
        dx_scr[pl.ds(rows + at, blk), :] = (dy.astype(F32) + rest_scr[pl.ds(at, blk), :]).astype(BF16)

    def block_of(scr, index):
        return scr[pl.ds(pl.multiple_of(index * blk, blk), blk), :]

    for n, scr in enumerate((out_scr, dx_scr)):
        for j in range(cap):
            send_ref[pl.ds((n * cap + j) * blk, blk), :] = block_of(scr, plan_ref[4 * n + j])
    for n, (scr, keep_ref) in enumerate(((out_scr, keep_f_ref), (dx_scr, keep_b_ref))):
        for k in range(4):
            keep_ref[pl.ds(k * blk, blk), :] = block_of(scr, jnp.minimum(plan_ref[8 + 4 * n + k], 7))


def make_rows(cap, first, tiles, plan, x, dy, got, low, low2, high, high2, up, down, g, late):
    rows, width = x.shape
    rank = up.shape[0]
    blk = rows // 4
    cols = tiles * TILE
    return pl.pallas_call(
        functools.partial(rows_kernel, cap, blk),
        grid=(tiles,),
        out_shape=(
            jax.ShapeDtypeStruct((2 * cap * blk, cols), BF16),
            jax.ShapeDtypeStruct((rows, cols), BF16),
            jax.ShapeDtypeStruct((rows, cols), BF16),
        ),
        in_specs=[
            SMEM, column(rows, first), column(rows, first), column(rows + 3 * blk),
            whole(low.shape), whole(low.shape), whole(high.shape), whole(high.shape),
            column(rank, first), pl.BlockSpec((TILE, rank), lambda i: (first + i, 0)), column(1, first),
        ] + [column(blk, first)] * (cap - 3),
        out_specs=(column(2 * cap * blk), column(rows), column(rows)),
        scratch_shapes=[
            pltpu.VMEM((2 * rows, TILE), BF16), pltpu.VMEM((2 * rows, TILE), BF16), pltpu.VMEM((rows, TILE), F32)
        ],
        compiler_params=ROOM,
        cost_estimate=FREE,
        name="rows",
    )(plan, x, dy, got, low, low2, high, high2, up, down, g, *[late] * (cap - 3))


def merge_kernel(cap, blk, spans, plan_ref, *refs):
    outs, sems = refs[-3:-1], refs[-1]
    waits = []
    for c, (first, cols) in enumerate(spans):
        keeps, got = refs[3 * c : 3 * c + 2], refs[3 * c + 2]
        for n in range(2):
            for k in range(4):
                index = plan_ref[8 + 4 * n + k]
                rows = pl.ds(k * blk, blk)
                to = outs[n].at[rows, pl.ds(first, cols)]
                sem = sems.at[8 * c + 4 * n + k]
                row = pl.multiple_of((n * cap + jnp.clip(index - 8, 0, cap - 1)) * blk, blk)
                here = pltpu.make_async_copy(keeps[n].at[rows, :], to, sem)
                there = pltpu.make_async_copy(got.at[pl.ds(row, blk), :], to, sem)

                @pl.when(index < 8)
                def _():
                    here.start()

                @pl.when(index >= 8)
                def _():
                    there.start()

                waits.append(here)
    for copy in waits:
        copy.wait()


def make_merge(cap, plan, parts):
    rows = parts[0][0].shape[0]
    spans, first = [], 0
    for keep_f, _, _ in parts:
        spans.append((first, keep_f.shape[1]))
        first += keep_f.shape[1]
    hbm = pl.BlockSpec(memory_space=pl.ANY)
    return pl.pallas_call(
        functools.partial(merge_kernel, cap, rows // 4, tuple(spans)),
        out_shape=(jax.ShapeDtypeStruct((rows, first), BF16),) * 2,
        in_specs=[SMEM] + [hbm] * (3 * len(parts)),
        out_specs=(hbm, hbm),
        scratch_shapes=[pltpu.SemaphoreType.DMA((8 * len(parts),))],
        compiler_params=ROOM,
        cost_estimate=FREE,
        name="merge",
    )(plan, *[array for part in parts for array in part])


def join_kernel(places, *refs):
    count = len(places)
    sems = refs[-1]
    outs = refs[-3:-1]
    parts = refs[-3 - 2 * count : -3]
    copies = []
    for n in range(2):
        for i, (first, cols) in enumerate(places):
            copies.append(
                pltpu.make_async_copy(parts[n * count + i], outs[n].at[:, pl.ds(first, cols)], sems.at[n * count + i])
            )
    for copy in copies:
        copy.start()
    for copy in copies:
        copy.wait()


def make_join(width, first, nexts, returns, into=()):
    rows = nexts[0].shape[0]
    places = []
    for part in nexts:
        places.append((first, part.shape[1]))
        first += part.shape[1]
    hbm = pl.BlockSpec(memory_space=pl.ANY)
    return pl.pallas_call(
        functools.partial(join_kernel, tuple(places)),
        out_shape=(jax.ShapeDtypeStruct((rows, width), BF16),) * 2,
        in_specs=[hbm] * (len(into) + 2 * len(nexts)),
        out_specs=(hbm, hbm),
        scratch_shapes=[pltpu.SemaphoreType.DMA((2 * len(nexts),))],
        input_output_aliases={i: i for i in range(len(into))},
        compiler_params=ROOM,
        cost_estimate=FREE,
        name="join",
    )(*into, *nexts, *returns)


VMEM = pl.BlockSpec(memory_space=pltpu.VMEM)


def grad_down_kernel(x_ref, low_ref, low2_ref, high_ref, high2_ref, g_ref, *refs):
    got_refs, to_ref = refs[:-1], refs[-1]
    rows = x_ref.shape[0]
    dpre = [(low[rows:, :].astype(F32) * 0.5).astype(BF16) for low in (low_ref, low2_ref)]
    rinv = [high[...].T[:, 0:1] for high in (high_ref, high2_ref)]
    first = 0
    for got_ref in got_refs:
        at = slice(first, first + got_ref.shape[1])
        first = at.stop
        g = g_ref[:, at]
        own = (x_ref[:, at].astype(F32) * rinv[0] * g).astype(BF16)
        other = (got_ref[:rows, :].astype(F32) * rinv[1] * g).astype(BF16)
        to_ref[at, :] = dot(own, dpre[0], ((0,), (0,))) + dot(other, dpre[1], ((0,), (0,)))


def make_grad_down(x, got, low, low2, high, high2, g):
    return pl.pallas_call(
        grad_down_kernel,
        out_shape=jax.ShapeDtypeStruct((x.shape[1], low.shape[1]), F32),
        in_specs=[VMEM] * (6 + len(got)),
        out_specs=VMEM,
        compiler_params=ROOM,
        cost_estimate=FREE,
        name="grad_down",
    )(x, low, low2, high, high2, g, *got)


def last_kernel(places, starts, plan_ref, low_ref, low2_ref, dy_ref, late_ref, *refs):
    chunks, count = len(starts) - 1, len(places)
    got_refs = refs[:chunks]
    parts = refs[chunks : chunks + 2 * count]
    to_ref, next_ref, return_ref = refs[chunks + 2 * count : chunks + 2 * count + 3]
    dy_scr, other_scr, to_scr, part_sems, in_sems, out_sems = refs[chunks + 2 * count + 3 :]
    rows = dy_ref.shape[0]
    blk = rows // 4
    loads, stores = [], []
    for c, got_ref in enumerate(got_refs):
        at = slice(starts[c], starts[c + 1])
        pairs = (
            (dy_ref.at[:, at], dy_scr.at[:, at]),
            (got_ref.at[pl.ds(rows, 3 * blk), :], other_scr.at[pl.ds(0, 3 * blk), at]),
            (late_ref.at[:, at], other_scr.at[pl.ds(3 * blk, blk), at]),
        )
        loads.append([pltpu.make_async_copy(x, y, in_sems.at[3 * c + n]) for n, (x, y) in enumerate(pairs)])
        stores.append(pltpu.make_async_copy(to_scr.at[:, at], to_ref.at[:, at], out_sems.at[c]))
    for some in loads:
        for copy in some:
            copy.start()
    joins = []
    for n, out_ref in enumerate((next_ref, return_ref)):
        for i, (first, cols) in enumerate(places):
            sem = part_sems.at[n * count + i]
            joins.append(pltpu.make_async_copy(parts[n * count + i], out_ref.at[:, pl.ds(first, cols)], sem))
    for copy in joins:
        copy.start()
    own = (low_ref[:rows, :].astype(F32) * 0.5).T.astype(BF16)
    ats = [pl.ds(pl.multiple_of(plan_ref[20 + j] * blk, blk), blk) for j in range(4)]
    other = jnp.concatenate([(low2_ref[at, :].astype(F32) * 0.5).T.astype(BF16) for at in ats], axis=1)
    for c, some in enumerate(loads):
        for copy in some:
            copy.wait()
        at = slice(starts[c], starts[c + 1])
        to_scr[:, at] = dot(own, dy_scr[:, at], ((1,), (0,))) + dot(other, other_scr[:, at], ((1,), (0,)))
        stores[c].start()
    for copy in joins + stores:
        copy.wait()


def make_last(plan, dy, late, got, low, low2, nexts, returns):
    rows, width = dy.shape
    rank = low.shape[1]
    starts, places = [0], []
    for block in got:
        starts.append(starts[-1] + block.shape[1])
    first = 0
    for part in nexts:
        places.append((first, part.shape[1]))
        first += part.shape[1]
    hbm = pl.BlockSpec(memory_space=pl.ANY)
    routed = jax.ShapeDtypeStruct((rows, width), BF16)
    return pl.pallas_call(
        functools.partial(last_kernel, tuple(places), tuple(starts)),
        out_shape=(jax.ShapeDtypeStruct((rank, width), F32), routed, routed),
        in_specs=[SMEM, VMEM, VMEM] + [hbm] * (2 + len(got) + 2 * len(nexts)),
        out_specs=(hbm,) * 3,
        scratch_shapes=[
            pltpu.VMEM((rows, width), BF16), pltpu.VMEM((rows, width), BF16), pltpu.VMEM((rank, width), F32),
            pltpu.SemaphoreType.DMA((2 * len(nexts),)), pltpu.SemaphoreType.DMA((3 * len(got),)),
            pltpu.SemaphoreType.DMA((len(got),)),
        ],
        compiler_params=ROOM,
        cost_estimate=FREE,
        name="last",
    )(plan, low, low2, dy, late, *got, *nexts, *returns)


def four_peers(inputs, out_grad, gains, down_proj, up_proj, wiring, pair_mask):
    x, dy, down, up = inputs[0, 0], out_grad[0, 0], down_proj[0], up_proj[0]
    width = x.shape[1]
    count = len(CHUNKS)
    starts = [sum(CHUNKS[:c]) for c in range(count + 1)]
    plan, choice, low, high, *outs, late = make_open(
        [n * TILE for n in CHUNKS], wiring, pair_mask, gains, x, dy, down, up
    )
    choice = choice[0]

    def stage(number, cap, mask, state):
        exchange, route = STAGES[number]
        if number == 0:
            held = {}
            late2 = swapped(late, "peer", mask) if cap == 4 else late
        else:
            low2, high2, late2, held = state
        held, parts, backs, sent = dict(held), [], {}, plan

        def send_on(c):
            ready = [source[d] for source, d in ((held, c - DEPTH), (backs, c - LAG)) if d in source]
            held[c] = swapped(after(outs[c], *ready) if ready else outs[c], "peer", mask)

        waiting = list(exchange)
        while waiting and (waiting[0] < exchange[0] + DEPTH):
            send_on(waiting.pop(0))
        if number == 0:
            low2, high2 = make_unpack(held[0], low, high)
        common = (low, low2, high, high2)
        for c in route:
            send, keep_f, keep_b = make_rows(
                cap, starts[c], CHUNKS[c], after(plan, sent), x, dy, held[c], *common, up, down, gains, late2
            )
            backs[c] = swapped(send, "peer", 1 if mask >= 2 else 2)
            parts.append((keep_f, keep_b, backs[c]))
            sent = send
            if waiting:
                send_on(waiting.pop(0))
        while waiting:
            send_on(waiting.pop(0))
        grads = ()
        if number == len(STAGES) - 1 and cap == 3:
            late2 = swapped(after(late, held[count - 1]), "peer", mask)
        if number == len(STAGES) - 1:
            blocks = [held[c] for c in range(count)]
            grads = make_grad_down(after(x, sent), blocks, *common, gains)
        merged = make_merge(cap, after(plan, sent), parts)
        return merged, (low2, high2) if number == 0 else (), late2, {c: held[c] for c in exchange}, grads

    state = None
    nexts, returns = [], []
    for number in range(len(STAGES)):
        branches = [functools.partial(stage, number, cap, m) for cap in (3, 4) for m in (1, 2, 3)]
        (f, b), made, late2, arrived, grad_down = lax.switch(choice, branches, state)
        if number == 0:
            low2, high2 = made
            held = {}
        held = {**held, **arrived}
        state = (low2, high2, late2, held)
        if number:
            f, b = after(f, nexts[-1], returns[-1]), after(b, nexts[-1], returns[-1])
        nexts.append(passed_along(f, "section", 1))
        returns.append(passed_along(b, "section", -1))
    grad_up, *joined = make_last(
        plan, after(dy, f, b), late2, [held[c] for c in range(count)], low, low2, nexts[:-1], returns[:-1]
    )
    done = sum(part.shape[1] for part in nexts[:-1])
    next_rows, return_rows = make_join(width, done, nexts[-1:], returns[-1:], into=joined)
    return next_rows[None, None], return_rows[None, None], grad_down[None, None], grad_up[None, None]


def adapter(x, dy, g, down, up):
    xf = x.astype(F32)
    rinv = lax.rsqrt(jnp.mean(xf * xf, axis=-1, keepdims=True) + 1e-05)
    normed = (xf * rinv * g).astype(BF16)
    pre = dot(normed, down, ((1,), (0,)))
    sig = jax.nn.sigmoid(pre)
    act = (pre * sig).astype(BF16)
    dact = dot(dy, up, ((1,), (1,)))
    dpre = (dact * sig * (1.0 + pre * (1.0 - sig))).astype(BF16)
    inner = jnp.sum(dpre.astype(F32) * pre, axis=-1, keepdims=True) / x.shape[1]
    return act, dpre, rinv, rinv * rinv * inner


def layer(x, dy, g, down, up):
    xf = x.astype(F32)
    act, dpre, rinv, weight = adapter(x, dy, g, down, up)
    normed = (xf * rinv * g).astype(BF16)
    out = (xf + dot(act, up, ((1,), (0,)))).astype(BF16)
    gup = dot(act, dy, ((0,), (0,))).astype(BF16)
    gdown = dot(normed, dpre, ((0,), (0,))).astype(BF16)
    dnorm = dot(dpre, down, ((1,), (1,))) * g
    dx = (dy.astype(F32) + rinv * dnorm - xf * weight).astype(BF16)
    return (out, dx, gdown, gup)


def pack_blocks(blocks, counts_vec, first_vec, slots):
    peers = counts_vec.shape[0]
    nblocks = blocks.shape[0]
    place = jnp.arange(slots, dtype=jnp.int32)
    source = first_vec[:, None] + place[None, :]
    valid = place[None, :] < counts_vec[:, None]
    select = (source[:, :, None] == jnp.arange(nblocks, dtype=jnp.int32)[None, None, :]) & valid[:, :, None]
    select = select.astype(BF16).reshape(peers * slots, nblocks)
    return jnp.dot(select, blocks, preferred_element_type=F32).astype(BF16)


def unpack_blocks(received, counts_vec, first_vec, slots, nblocks):
    place = jnp.arange(slots, dtype=jnp.int32)
    target = (first_vec[:, None] + place[None, :]).reshape(-1)
    valid = (place[None, :] < counts_vec[:, None]).reshape(-1)
    select = (target[None, :] == jnp.arange(nblocks, dtype=jnp.int32)[:, None]) & valid[None, :]
    return jnp.dot(select.astype(BF16), received, preferred_element_type=F32).astype(BF16)


def any_peers(inputs, out_grad, gains, down_proj, up_proj, wiring, pair_mask):
    sections = lax.axis_size("section")
    nblocks = lax.axis_size("peer")
    section = lax.axis_index("section")
    peer = lax.axis_index("peer")
    x = inputs[0, 0]
    rows, width = x.shape
    out, dx, gdown, gup = layer(x, out_grad[0, 0], gains[0], down_proj[0], up_proj[0])
    blk_rows = rows // nblocks
    here = lax.dynamic_index_in_dim(wiring, section, 0, keepdims=False)
    before = lax.dynamic_index_in_dim(wiring, (section + sections - 1) % sections, 0, keepdims=False)
    here_start = jnp.cumsum(here, axis=1) - here
    before_col = jnp.cumsum(before, axis=0) - before
    out_blocks = out.reshape(nblocks, blk_rows * width)
    dx_blocks = dx.reshape(nblocks, blk_rows * width)
    fwd_buf = pack_blocks(out_blocks, here[peer], here_start[peer], CAP)
    back_buf = pack_blocks(dx_blocks, before[:, peer], before_col[:, peer], CAP)
    moved = passed_along(fwd_buf, "section", 1)
    got_fwd = lax.all_to_all(moved, "peer", split_axis=0, concat_axis=0, tiled=True)
    next_rows = unpack_blocks(got_fwd, before[:, peer], before_col[:, peer], CAP, nblocks)
    moved_back = passed_along(back_buf, "section", -1)
    got_back = lax.all_to_all(moved_back, "peer", split_axis=0, concat_axis=0, tiled=True)
    return_rows = unpack_blocks(got_back, here[peer], here_start[peer], CAP, nblocks)
    mask_value = pair_mask[section]
    other_down, other_up = (gdown, gup)
    for bit in range(nblocks.bit_length() - 1):
        swapped_down, swapped_up = swapped((other_down, other_up), "peer", 1 << bit)
        take = jnp.bitwise_and(jnp.right_shift(mask_value, bit), 1) == 1
        other_down = jnp.where(take, swapped_down, other_down)
        other_up = jnp.where(take, swapped_up, other_up)
    grad_down = (gdown.astype(F32) + other_down.astype(F32)) * 0.5
    grad_up = (gup.astype(F32) + other_up.astype(F32)) * 0.5
    return (
        next_rows.reshape(1, 1, rows, width),
        return_rows.reshape(1, 1, rows, width),
        grad_down[None, None],
        grad_up[None, None],
    )


def solution(mesh):
    whole = P("section", "peer", None, None)
    return jax.shard_map(
        four_peers if mesh.shape["peer"] == 4 else any_peers,
        mesh=mesh,
        in_specs=(whole, whole, P("section", None), P("section", None, None), P("section", None, None), P(), P()),
        out_specs=(whole,) * 4,
        check_vma=False,
    )
```

```python
import functools

import jax
import jax.numpy as jnp
from jax import lax
from jax.experimental import pallas as pl
from jax.experimental.pallas import tpu as pltpu
from jax.sharding import PartitionSpec as P

CAP = 2
TILE = 512
CHUNKS = (1, 2, 3, 2, 2)
STAGES = (((0, 1, 2), (0, 1)), ((3, 4), (2, 3)), ((), (4,)))
DEPTH, LAG = 2, 3
F32, BF16 = jnp.float32, jnp.bfloat16


def passed_along(block, axis, distance):
    devices = range(lax.axis_size(axis))
    route = [((i - distance) % len(devices), i) for i in devices]
    return lax.ppermute(block, axis, route)


def swapped(block, axis, mask):
    count = lax.axis_size(axis)
    return lax.ppermute(block, axis, [(i, i ^ mask) for i in range(count) if i ^ mask < count])


def after(value, *others):
    return lax.optimization_barrier((value, *others))[0]


def dot(a, b, dims):
    return lax.dot_general(a, b, (dims, ((), ())), preferred_element_type=F32)


PIECE = 1024
FREE = pl.CostEstimate(flops=0, bytes_accessed=0, transcendentals=0)
ROOM = pltpu.CompilerParams(vmem_limit_bytes=32 * 2**20)
SMEM = pl.BlockSpec(memory_space=pltpu.SMEM)


def open_kernel(widths, wiring_ref, mask_ref, g_ref, x_ref, dy_ref, down_ref, up_ref, plan_ref, choice_ref, low_ref,
                high_ref, *refs):
    outs, late_ref = refs[: len(widths)], refs[len(widths)]
    x_scr, dy_scr, down_scr, up_scr, extra, in_sems, out_sems, extra_sems = refs[len(widths) + 1 :]
    rows, width = x_ref.shape
    rank = up_ref.shape[0]
    pieces = [slice(i, i + PIECE) for i in range(0, width, PIECE)]
    loads = []
    for i, at in enumerate(pieces):
        pairs = ((x_ref.at[:, at], x_scr.at[:, at]), (dy_ref.at[:, at], dy_scr.at[:, at]),
                 (down_ref.at[at, :], down_scr.at[at, :]), (up_ref.at[:, at], up_scr.at[:, at]))
        loads.append([pltpu.make_async_copy(s, t, in_sems.at[4 * i + n]) for n, (s, t) in enumerate(pairs)])
    for some in loads:
        for copy in some:
            copy.start()
    section, peer = lax.axis_index("section"), lax.axis_index("peer")
    count = wiring_ref.shape[0]
    before = lax.rem(section + count - 1, count)
    mask = mask_ref[section]
    match = peer ^ mask
    other = peer ^ jnp.where(mask >= 2, 1, 2)

    def sources(back, q):
        at = [jnp.int32(0)] * 4
        block = [jnp.int32(0)] * 4
        cum = jnp.int32(0)
        for i in range(4):
            first = jnp.int32(0)
            for j in range(4):
                if back:
                    first += jnp.where(j < q, wiring_ref[before, j, i], 0)
                else:
                    first += jnp.where(j < q, wiring_ref[section, i, j], 0)
            amount = wiring_ref[before, q, i] if back else wiring_ref[section, i, q]
            for k in range(4):
                inside = (cum <= k) & (k < cum + amount)
                at[k] = jnp.where(inside, i, at[k])
                block[k] = jnp.where(inside, first + k - cum, block[k])
            cum += amount
        held = [((a == peer) | (a == match)).astype(jnp.int32) for a in at]
        index = [jnp.where(a == peer, b, 4 + b) for a, b in zip(at, block)]
        return held, index

    for n, back in enumerate((False, True)):
        held, index = sources(back, other)
        order = jnp.int32(0)
        orders = []
        for k in range(4):
            orders.append(order)
            order += held[k]
        for j in range(4):
            pick = jnp.int32(0)
            for k in range(4):
                pick += jnp.where((held[k] == 1) & (orders[k] == j), index[k], 0)
            plan_ref[4 * n + j] = pick
        held, index = sources(back, peer)
        order = jnp.int32(0)
        for k in range(4):
            plan_ref[8 + 4 * n + k] = jnp.where(held[k] == 1, index[k], 8 + order)
            order += 1 - held[k]
    twos = jnp.int32(0)
    for at in (section, before):
        for i in range(4):
            for j in range(4):
                twos += jnp.where(wiring_ref[at, i, j] == 2, 1, 0)
    choice_ref[0] = mask - 1 + jnp.where(twos > 8, 3, 0)
    for n, (owner, to) in enumerate(((peer, match), (match, peer))):
        wanted, cum = [jnp.int32(0)] * 4, jnp.int32(0)
        for q in range(4):
            amount = wiring_ref[before, q, owner]
            near = ((q == to) | (q == (to ^ jnp.where(mask >= 2, 1, 2)))).astype(jnp.int32)
            for k in range(4):
                wanted[k] = jnp.where((cum <= k) & (k < cum + amount), near, wanted[k])
            cum += amount
        total = sum(wanted)
        ahead, behind = jnp.int32(0), jnp.int32(0)
        slots = []
        for k in range(4):
            slots.append(jnp.where(wanted[k] == 1, ahead, total + behind))
            ahead += wanted[k]
            behind += 1 - wanted[k]
        for j in range(4):
            plan_ref[16 + 4 * n + j] = sum(jnp.where(slots[k] == j, k, 0) for k in range(4))

    blk = rows // 4
    stores, first = [], 0
    for c, cols in enumerate(widths):
        at = pl.ds(first, cols)
        first += cols
        sem = out_sems.at[4 * c]
        stores.append((first, pltpu.make_async_copy(x_scr.at[:, at], outs[c].at[pl.ds(0, rows), :], sem)))
        for j in range(3):
            from_rows = pl.ds(pl.multiple_of(plan_ref[16 + j] * blk, blk), blk)
            to = outs[c].at[pl.ds(rows + j * blk, blk), :]
            stores.append((first, pltpu.make_async_copy(dy_scr.at[from_rows, at], to, out_sems.at[4 * c + 1 + j])))
    from_rows = pl.ds(pl.multiple_of(plan_ref[19] * blk, blk), blk)
    stores.append((width, pltpu.make_async_copy(dy_scr.at[from_rows, :], late_ref, extra_sems.at[1])))

    square = jnp.zeros((rows, 1), F32)
    pre = jnp.zeros((rows, rank), F32)
    dact = jnp.zeros((rows, rank), F32)
    for some, at in zip(loads, pieces):
        for copy in some:
            copy.wait()
        for end, copy in stores:
            if at.start < end <= at.stop:
                copy.start()
        x = x_scr[:, at].astype(F32)
        square += jnp.sum(x * x, axis=1, keepdims=True)
        dact += dot(dy_scr[:, at], up_scr[:, at], ((1,), (1,)))
    rinv = lax.rsqrt(square / width + 1e-05)
    for at in pieces:
        normed = (x_scr[:, at].astype(F32) * rinv * g_ref[:, at]).astype(BF16)
        pre += dot(normed, down_scr[at, :], ((1,), (0,)))
    v = pre
    sig = jax.nn.sigmoid(v)
    act = (v * sig).astype(BF16)
    dpre = (dact * sig * (1.0 + v * (1.0 - sig))).astype(BF16)
    inner = jnp.sum(dpre.astype(F32) * v, axis=1, keepdims=True) / width
    weight = rinv * rinv * inner
    low_ref[:rows, :] = act
    low_ref[rows:, :] = dpre
    lane = lax.broadcasted_iota(jnp.int32, (rows, rows), 1)
    high = jnp.where(lane == 0, rinv, weight).T[:8, :]
    high_ref[...] = high
    bands = widths[0] // rank
    band = 2 * rows // bands
    for j in range(bands):
        from_ref = act if (j + 1) * band <= rows else dpre
        start = j * band % rows
        extra[:band, j * rank : (j + 1) * rank] = from_ref[start : start + band, :]
    rest = high
    parts = []
    for _ in range(3):
        part = rest.astype(BF16)
        parts.append(part)
        rest = rest - part.astype(F32)
    extra[band:, :] = jnp.zeros_like(extra[band:, :])
    extra[band : band + 16, 0:rows] = jnp.concatenate([parts[0], parts[1]], axis=0)
    extra[band : band + 16, rows : 2 * rows] = jnp.concatenate([parts[2], parts[2]], axis=0)
    last = pltpu.make_async_copy(extra, outs[0].at[pl.ds(rows + 3 * blk, band + 16), :], extra_sems.at[0])
    last.start()
    for _, copy in stores:
        copy.wait()
    last.wait()


def make_open(widths, wiring, pair_mask, g, x, dy, down, up):
    rows, width = x.shape
    rank = up.shape[0]
    band = 2 * rows * rank // widths[0]
    hbm = pl.BlockSpec(memory_space=pl.ANY)
    vmem = pl.BlockSpec(memory_space=pltpu.VMEM)
    sent = rows + 3 * (rows // 4)
    tall = [sent + band + 16] + [sent] * (len(widths) - 1)
    return pl.pallas_call(
        functools.partial(open_kernel, widths),
        out_shape=[
            jax.ShapeDtypeStruct((24,), jnp.int32),
            jax.ShapeDtypeStruct((1,), jnp.int32),
            jax.ShapeDtypeStruct((2 * rows, rank), BF16),
            jax.ShapeDtypeStruct((8, rows), F32),
        ] + [jax.ShapeDtypeStruct((n, cols), BF16) for n, cols in zip(tall, widths)]
        + [jax.ShapeDtypeStruct((rows // 4, width), BF16)],
        in_specs=[SMEM, SMEM, vmem, hbm, hbm, hbm, hbm],
        out_specs=[SMEM, SMEM, vmem, vmem] + [hbm] * (len(widths) + 1),
        scratch_shapes=[
            pltpu.VMEM((rows, width), BF16), pltpu.VMEM((rows, width), BF16),
            pltpu.VMEM((width, rank), BF16), pltpu.VMEM((rank, width), BF16),
            pltpu.VMEM((band + 16, widths[0]), BF16),
            pltpu.SemaphoreType.DMA((4 * (width // PIECE),)), pltpu.SemaphoreType.DMA((4 * len(widths),)),
            pltpu.SemaphoreType.DMA((2,)),
        ],
        compiler_params=ROOM,
        cost_estimate=FREE,
        name="open",
    )(wiring, pair_mask, g, x, dy, down, up)


def unpack_kernel(got_ref, low_ref, high_ref):
    rows2, rank = low_ref.shape
    bands = got_ref.shape[1] // rank
    band = rows2 // bands
    rows = rows2 // 2
    first = got_ref.shape[0] - band - 16
    for j in range(bands):
        low_ref[j * band : (j + 1) * band, :] = got_ref[first : first + band, j * rank : (j + 1) * rank]
    parts = got_ref[first + band :, :].astype(F32)
    high_ref[...] = parts[0:8, 0:rows] + parts[8:16, 0:rows] + parts[0:8, rows : 2 * rows]


def make_unpack(got, low, high):
    vmem = pl.BlockSpec(memory_space=pltpu.VMEM)
    return pl.pallas_call(
        unpack_kernel,
        out_shape=(jax.ShapeDtypeStruct(low.shape, BF16), jax.ShapeDtypeStruct(high.shape, F32)),
        in_specs=[vmem],
        out_specs=(vmem, vmem),
        compiler_params=ROOM,
        cost_estimate=FREE,
        name="unpack",
    )(got)


def whole(shape):
    return pl.BlockSpec(shape, lambda i: (0,) * len(shape))


def column(rows, first=0, tile=TILE):
    return pl.BlockSpec((rows, tile), lambda i: (0, first + i))


def chunk(rows, start, end, tile=TILE):
    return pl.BlockSpec((rows, tile), lambda i: (0, jnp.clip(i - start, 0, end - start - 1)))


def rows_kernel(cap, blk, plan_ref, x_ref, dy_ref, got_ref, low_ref, low2_ref, high_ref, high2_ref, up_ref, down_ref,
                g_ref, *refs):
    late_refs = refs[: cap - 3]
    send_ref, keep_f_ref, keep_b_ref, out_scr, dx_scr, rest_scr = refs[cap - 3 :]
    rows = x_ref.shape[0]
    for half in range(2):
        part = pl.ds(half * rows, rows)
        x = (x_ref[...] if half == 0 else got_ref[:rows, :]).astype(F32)
        low = low_ref if half == 0 else low2_ref
        stat = (high_ref if half == 0 else high2_ref)[...].T
        out = x + dot(low[:rows, :], up_ref[...], ((1,), (0,)))
        out_scr[part, :] = out.astype(BF16)
        dn = dot(low[rows:, :], down_ref[...], ((1,), (1,))) * g_ref[...]
        rest = stat[:, 0:1] * dn - x * stat[:, 1:2]
        if half == 0:
            dx_scr[part, :] = (dy_ref[...].astype(F32) + rest).astype(BF16)
        else:
            rest_scr[...] = rest
    for j in range(cap):
        dy = late_refs[0][...] if j == 3 else got_ref[rows + j * blk : rows + (j + 1) * blk, :]
        at = pl.multiple_of(plan_ref[20 + j] * blk, blk)
        dx_scr[pl.ds(rows + at, blk), :] = (dy.astype(F32) + rest_scr[pl.ds(at, blk), :]).astype(BF16)

    def block_of(scr, index):
        return scr[pl.ds(pl.multiple_of(index * blk, blk), blk), :]

    for n, scr in enumerate((out_scr, dx_scr)):
        for j in range(cap):
            send_ref[pl.ds((n * cap + j) * blk, blk), :] = block_of(scr, plan_ref[4 * n + j])
    for n, (scr, keep_ref) in enumerate(((out_scr, keep_f_ref), (dx_scr, keep_b_ref))):
        for k in range(4):
            keep_ref[pl.ds(k * blk, blk), :] = block_of(scr, jnp.minimum(plan_ref[8 + 4 * n + k], 7))


def make_rows(cap, first, tiles, plan, x, dy, got, low, low2, high, high2, up, down, g, late):
    rows, width = x.shape
    rank = up.shape[0]
    blk = rows // 4
    cols = tiles * TILE
    return pl.pallas_call(
        functools.partial(rows_kernel, cap, blk),
        grid=(tiles,),
        out_shape=(
            jax.ShapeDtypeStruct((2 * cap * blk, cols), BF16),
            jax.ShapeDtypeStruct((rows, cols), BF16),
            jax.ShapeDtypeStruct((rows, cols), BF16),
        ),
        in_specs=[
            SMEM, column(rows, first), column(rows, first), column(rows + 3 * blk),
            whole(low.shape), whole(low.shape), whole(high.shape), whole(high.shape),
            column(rank, first), pl.BlockSpec((TILE, rank), lambda i: (first + i, 0)), column(1, first),
        ] + [column(blk, first)] * (cap - 3),
        out_specs=(column(2 * cap * blk), column(rows), column(rows)),
        scratch_shapes=[
            pltpu.VMEM((2 * rows, TILE), BF16), pltpu.VMEM((2 * rows, TILE), BF16), pltpu.VMEM((rows, TILE), F32)
        ],
        compiler_params=ROOM,
        cost_estimate=FREE,
        name="rows",
    )(plan, x, dy, got, low, low2, high, high2, up, down, g, *[late] * (cap - 3))


def merge_kernel(cap, blk, spans, plan_ref, *refs):
    outs, sems = refs[-3:-1], refs[-1]
    waits = []
    for c, (first, cols) in enumerate(spans):
        keeps, got = refs[3 * c : 3 * c + 2], refs[3 * c + 2]
        for n in range(2):
            for k in range(4):
                index = plan_ref[8 + 4 * n + k]
                rows = pl.ds(k * blk, blk)
                to = outs[n].at[rows, pl.ds(first, cols)]
                sem = sems.at[8 * c + 4 * n + k]
                row = pl.multiple_of((n * cap + jnp.clip(index - 8, 0, cap - 1)) * blk, blk)
                here = pltpu.make_async_copy(keeps[n].at[rows, :], to, sem)
                there = pltpu.make_async_copy(got.at[pl.ds(row, blk), :], to, sem)

                @pl.when(index < 8)
                def _():
                    here.start()

                @pl.when(index >= 8)
                def _():
                    there.start()

                waits.append(here)
    for copy in waits:
        copy.wait()


def make_merge(cap, plan, parts):
    rows = parts[0][0].shape[0]
    spans, first = [], 0
    for keep_f, _, _ in parts:
        spans.append((first, keep_f.shape[1]))
        first += keep_f.shape[1]
    hbm = pl.BlockSpec(memory_space=pl.ANY)
    return pl.pallas_call(
        functools.partial(merge_kernel, cap, rows // 4, tuple(spans)),
        out_shape=(jax.ShapeDtypeStruct((rows, first), BF16),) * 2,
        in_specs=[SMEM] + [hbm] * (3 * len(parts)),
        out_specs=(hbm, hbm),
        scratch_shapes=[pltpu.SemaphoreType.DMA((8 * len(parts),))],
        compiler_params=ROOM,
        cost_estimate=FREE,
        name="merge",
    )(plan, *[array for part in parts for array in part])


def join_kernel(places, *refs):
    count = len(places)
    sems = refs[-1]
    outs = refs[-3:-1]
    parts = refs[-3 - 2 * count : -3]
    copies = []
    for n in range(2):
        for i, (first, cols) in enumerate(places):
            copies.append(
                pltpu.make_async_copy(parts[n * count + i], outs[n].at[:, pl.ds(first, cols)], sems.at[n * count + i])
            )
    for copy in copies:
        copy.start()
    for copy in copies:
        copy.wait()


def make_join(width, first, nexts, returns, into=()):
    rows = nexts[0].shape[0]
    places = []
    for part in nexts:
        places.append((first, part.shape[1]))
        first += part.shape[1]
    hbm = pl.BlockSpec(memory_space=pl.ANY)
    return pl.pallas_call(
        functools.partial(join_kernel, tuple(places)),
        out_shape=(jax.ShapeDtypeStruct((rows, width), BF16),) * 2,
        in_specs=[hbm] * (len(into) + 2 * len(nexts)),
        out_specs=(hbm, hbm),
        scratch_shapes=[pltpu.SemaphoreType.DMA((2 * len(nexts),))],
        input_output_aliases={i: i for i in range(len(into))},
        compiler_params=ROOM,
        cost_estimate=FREE,
        name="join",
    )(*into, *nexts, *returns)


VMEM = pl.BlockSpec(memory_space=pltpu.VMEM)


def grad_down_kernel(x_ref, low_ref, low2_ref, high_ref, high2_ref, g_ref, *refs):
    got_refs, to_ref = refs[:-1], refs[-1]
    rows = x_ref.shape[0]
    dpre = [(low[rows:, :].astype(F32) * 0.5).astype(BF16) for low in (low_ref, low2_ref)]
    rinv = [high[...].T[:, 0:1] for high in (high_ref, high2_ref)]
    first = 0
    for got_ref in got_refs:
        at = slice(first, first + got_ref.shape[1])
        first = at.stop
        g = g_ref[:, at]
        own = (x_ref[:, at].astype(F32) * rinv[0] * g).astype(BF16)
        other = (got_ref[:rows, :].astype(F32) * rinv[1] * g).astype(BF16)
        to_ref[at, :] = dot(own, dpre[0], ((0,), (0,))) + dot(other, dpre[1], ((0,), (0,)))


def make_grad_down(x, got, low, low2, high, high2, g):
    return pl.pallas_call(
        grad_down_kernel,
        out_shape=jax.ShapeDtypeStruct((x.shape[1], low.shape[1]), F32),
        in_specs=[VMEM] * (6 + len(got)),
        out_specs=VMEM,
        compiler_params=ROOM,
        cost_estimate=FREE,
        name="grad_down",
    )(x, low, low2, high, high2, g, *got)


def last_kernel(places, starts, plan_ref, low_ref, low2_ref, dy_ref, late_ref, *refs):
    chunks, count = len(starts) - 1, len(places)
    got_refs = refs[:chunks]
    parts = refs[chunks : chunks + 2 * count]
    to_ref, next_ref, return_ref = refs[chunks + 2 * count : chunks + 2 * count + 3]
    dy_scr, other_scr, to_scr, part_sems, in_sems, out_sems = refs[chunks + 2 * count + 3 :]
    rows = dy_ref.shape[0]
    blk = rows // 4
    loads, stores = [], []
    for c, got_ref in enumerate(got_refs):
        at = slice(starts[c], starts[c + 1])
        pairs = (
            (dy_ref.at[:, at], dy_scr.at[:, at]),
            (got_ref.at[pl.ds(rows, 3 * blk), :], other_scr.at[pl.ds(0, 3 * blk), at]),
            (late_ref.at[:, at], other_scr.at[pl.ds(3 * blk, blk), at]),
        )
        loads.append([pltpu.make_async_copy(x, y, in_sems.at[3 * c + n]) for n, (x, y) in enumerate(pairs)])
        stores.append(pltpu.make_async_copy(to_scr.at[:, at], to_ref.at[:, at], out_sems.at[c]))
    for some in loads:
        for copy in some:
            copy.start()
    joins = []
    for n, out_ref in enumerate((next_ref, return_ref)):
        for i, (first, cols) in enumerate(places):
            sem = part_sems.at[n * count + i]
            joins.append(pltpu.make_async_copy(parts[n * count + i], out_ref.at[:, pl.ds(first, cols)], sem))
    for copy in joins:
        copy.start()
    own = (low_ref[:rows, :].astype(F32) * 0.5).T.astype(BF16)
    ats = [pl.ds(pl.multiple_of(plan_ref[20 + j] * blk, blk), blk) for j in range(4)]
    other = jnp.concatenate([(low2_ref[at, :].astype(F32) * 0.5).T.astype(BF16) for at in ats], axis=1)
    for c, some in enumerate(loads):
        for copy in some:
            copy.wait()
        at = slice(starts[c], starts[c + 1])
        to_scr[:, at] = dot(own, dy_scr[:, at], ((1,), (0,))) + dot(other, other_scr[:, at], ((1,), (0,)))
        stores[c].start()
    for copy in joins + stores:
        copy.wait()


def make_last(plan, dy, late, got, low, low2, nexts, returns):
    rows, width = dy.shape
    rank = low.shape[1]
    starts, places = [0], []
    for block in got:
        starts.append(starts[-1] + block.shape[1])
    first = 0
    for part in nexts:
        places.append((first, part.shape[1]))
        first += part.shape[1]
    hbm = pl.BlockSpec(memory_space=pl.ANY)
    routed = jax.ShapeDtypeStruct((rows, width), BF16)
    return pl.pallas_call(
        functools.partial(last_kernel, tuple(places), tuple(starts)),
        out_shape=(jax.ShapeDtypeStruct((rank, width), F32), routed, routed),
        in_specs=[SMEM, VMEM, VMEM] + [hbm] * (2 + len(got) + 2 * len(nexts)),
        out_specs=(hbm,) * 3,
        scratch_shapes=[
            pltpu.VMEM((rows, width), BF16), pltpu.VMEM((rows, width), BF16), pltpu.VMEM((rank, width), F32),
            pltpu.SemaphoreType.DMA((2 * len(nexts),)), pltpu.SemaphoreType.DMA((3 * len(got),)),
            pltpu.SemaphoreType.DMA((len(got),)),
        ],
        compiler_params=ROOM,
        cost_estimate=FREE,
        name="last",
    )(plan, low, low2, dy, late, *got, *nexts, *returns)


def four_peers(inputs, out_grad, gains, down_proj, up_proj, wiring, pair_mask):
    x, dy, down, up = inputs[0, 0], out_grad[0, 0], down_proj[0], up_proj[0]
    width = x.shape[1]
    count = len(CHUNKS)
    starts = [sum(CHUNKS[:c]) for c in range(count + 1)]
    plan, choice, low, high, *outs, late = make_open(
        [n * TILE for n in CHUNKS], wiring, pair_mask, gains, x, dy, down, up
    )
    choice = choice[0]

    def stage(number, cap, mask, state):
        exchange, route = STAGES[number]
        if number == 0:
            held = {}
            late2 = swapped(late, "peer", mask) if cap == 4 else late
        else:
            low2, high2, late2, held = state
        held, parts, backs, sent = dict(held), [], {}, plan

        def send_on(c):
            ready = [source[d] for source, d in ((held, c - DEPTH), (backs, c - LAG)) if d in source]
            held[c] = swapped(after(outs[c], *ready) if ready else outs[c], "peer", mask)

        waiting = list(exchange)
        while waiting and (waiting[0] < exchange[0] + DEPTH):
            send_on(waiting.pop(0))
        if number == 0:
            low2, high2 = make_unpack(held[0], low, high)
        common = (low, low2, high, high2)
        for c in route:
            send, keep_f, keep_b = make_rows(
                cap, starts[c], CHUNKS[c], after(plan, sent), x, dy, held[c], *common, up, down, gains, late2
            )
            backs[c] = swapped(send, "peer", 1 if mask >= 2 else 2)
            parts.append((keep_f, keep_b, backs[c]))
            sent = send
            if waiting:
                send_on(waiting.pop(0))
        while waiting:
            send_on(waiting.pop(0))
        grads = ()
        if number == len(STAGES) - 1 and cap == 3:
            late2 = swapped(after(late, held[count - 1]), "peer", mask)
        if number == len(STAGES) - 1:
            blocks = [held[c] for c in range(count)]
            grads = make_grad_down(after(x, sent), blocks, *common, gains)
        merged = make_merge(cap, after(plan, sent), parts)
        return merged, (low2, high2) if number == 0 else (), late2, {c: held[c] for c in exchange}, grads

    state = None
    nexts, returns = [], []
    for number in range(len(STAGES)):
        branches = [functools.partial(stage, number, cap, m) for cap in (3, 4) for m in (1, 2, 3)]
        (f, b), made, late2, arrived, grad_down = lax.switch(choice, branches, state)
        if number == 0:
            low2, high2 = made
            held = {}
        held = {**held, **arrived}
        state = (low2, high2, late2, held)
        if number:
            f, b = after(f, nexts[-1], returns[-1]), after(b, nexts[-1], returns[-1])
        nexts.append(passed_along(f, "section", 1))
        returns.append(passed_along(b, "section", -1))
    grad_up, *joined = make_last(
        plan, after(dy, f, b), late2, [held[c] for c in range(count)], low, low2, nexts[:-1], returns[:-1]
    )
    done = sum(part.shape[1] for part in nexts[:-1])
    next_rows, return_rows = make_join(width, done, nexts[-1:], returns[-1:], into=joined)
    return next_rows[None, None], return_rows[None, None], grad_down[None, None], grad_up[None, None]


def adapter(x, dy, g, down, up):
    xf = x.astype(F32)
    rinv = lax.rsqrt(jnp.mean(xf * xf, axis=-1, keepdims=True) + 1e-05)
    normed = (xf * rinv * g).astype(BF16)
    pre = dot(normed, down, ((1,), (0,)))
    sig = jax.nn.sigmoid(pre)
    act = (pre * sig).astype(BF16)
    dact = dot(dy, up, ((1,), (1,)))
    dpre = (dact * sig * (1.0 + pre * (1.0 - sig))).astype(BF16)
    inner = jnp.sum(dpre.astype(F32) * pre, axis=-1, keepdims=True) / x.shape[1]
    return act, dpre, rinv, rinv * rinv * inner


def layer(x, dy, g, down, up):
    xf = x.astype(F32)
    act, dpre, rinv, weight = adapter(x, dy, g, down, up)
    normed = (xf * rinv * g).astype(BF16)
    out = (xf + dot(act, up, ((1,), (0,)))).astype(BF16)
    gup = dot(act, dy, ((0,), (0,))).astype(BF16)
    gdown = dot(normed, dpre, ((0,), (0,))).astype(BF16)
    dnorm = dot(dpre, down, ((1,), (1,))) * g
    dx = (dy.astype(F32) + rinv * dnorm - xf * weight).astype(BF16)
    return (out, dx, gdown, gup)


def pack_blocks(blocks, counts_vec, first_vec, slots):
    peers = counts_vec.shape[0]
    nblocks = blocks.shape[0]
    place = jnp.arange(slots, dtype=jnp.int32)
    source = first_vec[:, None] + place[None, :]
    valid = place[None, :] < counts_vec[:, None]
    select = (source[:, :, None] == jnp.arange(nblocks, dtype=jnp.int32)[None, None, :]) & valid[:, :, None]
    select = select.astype(BF16).reshape(peers * slots, nblocks)
    return jnp.dot(select, blocks, preferred_element_type=F32).astype(BF16)


def unpack_blocks(received, counts_vec, first_vec, slots, nblocks):
    place = jnp.arange(slots, dtype=jnp.int32)
    target = (first_vec[:, None] + place[None, :]).reshape(-1)
    valid = (place[None, :] < counts_vec[:, None]).reshape(-1)
    select = (target[None, :] == jnp.arange(nblocks, dtype=jnp.int32)[:, None]) & valid[None, :]
    return jnp.dot(select.astype(BF16), received, preferred_element_type=F32).astype(BF16)


def any_peers(inputs, out_grad, gains, down_proj, up_proj, wiring, pair_mask):
    sections = lax.axis_size("section")
    nblocks = lax.axis_size("peer")
    section = lax.axis_index("section")
    peer = lax.axis_index("peer")
    x = inputs[0, 0]
    rows, width = x.shape
    out, dx, gdown, gup = layer(x, out_grad[0, 0], gains[0], down_proj[0], up_proj[0])
    blk_rows = rows // nblocks
    here = lax.dynamic_index_in_dim(wiring, section, 0, keepdims=False)
    before = lax.dynamic_index_in_dim(wiring, (section + sections - 1) % sections, 0, keepdims=False)
    here_start = jnp.cumsum(here, axis=1) - here
    before_col = jnp.cumsum(before, axis=0) - before
    out_blocks = out.reshape(nblocks, blk_rows * width)
    dx_blocks = dx.reshape(nblocks, blk_rows * width)
    fwd_buf = pack_blocks(out_blocks, here[peer], here_start[peer], CAP)
    back_buf = pack_blocks(dx_blocks, before[:, peer], before_col[:, peer], CAP)
    moved = passed_along(fwd_buf, "section", 1)
    got_fwd = lax.all_to_all(moved, "peer", split_axis=0, concat_axis=0, tiled=True)
    next_rows = unpack_blocks(got_fwd, before[:, peer], before_col[:, peer], CAP, nblocks)
    moved_back = passed_along(back_buf, "section", -1)
    got_back = lax.all_to_all(moved_back, "peer", split_axis=0, concat_axis=0, tiled=True)
    return_rows = unpack_blocks(got_back, here[peer], here_start[peer], CAP, nblocks)
    mask_value = pair_mask[section]
    other_down, other_up = (gdown, gup)
    for bit in range(nblocks.bit_length() - 1):
        swapped_down, swapped_up = swapped((other_down, other_up), "peer", 1 << bit)
        take = jnp.bitwise_and(jnp.right_shift(mask_value, bit), 1) == 1
        other_down = jnp.where(take, swapped_down, other_down)
        other_up = jnp.where(take, swapped_up, other_up)
    grad_down = (gdown.astype(F32) + other_down.astype(F32)) * 0.5
    grad_up = (gup.astype(F32) + other_up.astype(F32)) * 0.5
    return (
        next_rows.reshape(1, 1, rows, width),
        return_rows.reshape(1, 1, rows, width),
        grad_down[None, None],
        grad_up[None, None],
    )


def solution(mesh):
    whole = P("section", "peer", None, None)
    return jax.shard_map(
        four_peers if mesh.shape["peer"] == 4 else any_peers,
        mesh=mesh,
        in_specs=(whole, whole, P("section", None), P("section", None, None), P("section", None, None), P(), P()),
        out_specs=(whole,) * 4,
        check_vma=False,
    )
```
